32 devices in a mesh: seq: 4 (over x, core), dp: 8 (over z, y).
Axes of the slice: x: 2, y: 2, z: 4, core: 2. Of those that a mesh axis runs over, the one named last changes fastest.
Arguments:
- block_input: bfloat16 [8, 1024, 2048], P('dp', 'seq'), may hold values from -6 to 6
- out_grad: bfloat16 [8, 1024, 2048], P('dp', 'seq'), may hold values from -6 to 6
- lengths: int32 [8, 2], P('dp'), may hold values from 128 to 896, as said below
- vectors: float32 [16, 2048], P(None, ('seq', 'dp')), may hold values from -12 to 3, as said below
- vectors_moment: float32 [16, 2048], P(None, ('seq', 'dp')), may hold values from -28 to 28
- vectors_average: float32 [16, 2048], P(None, ('seq', 'dp')), may hold values from -3 to 3
- mix_weights: float32 [5, 2048, 2048], P(None, ('seq', 'dp')), may hold values from -0.125 to 0.125
- mix_moment: float32 [5, 2048, 2048], P(None, ('seq', 'dp')), may hold values from -5 to 5
- mix_average: float32 [5, 2048, 2048], P(None, ('seq', 'dp')), may hold values from -0.125 to 0.125
- ffn_key: float32 [2048, 7168], P(('seq', 'dp')), may hold values from -0.125 to 0.125
- ffn_key_moment: float32 [2048, 7168], P(('seq', 'dp')), may hold values from -5 to 5
- ffn_key_average: float32 [2048, 7168], P(('seq', 'dp')), may hold values from -0.125 to 0.125
- ffn_recept: float32 [2048, 2048], P(('seq', 'dp')), may hold values from -0.125 to 0.125
- ffn_recept_moment: float32 [2048, 2048], P(('seq', 'dp')), may hold values from -5 to 5
- ffn_recept_average: float32 [2048, 2048], P(('seq', 'dp')), may hold values from -0.125 to 0.125
- ffn_value: float32 [7168, 2048], P(('seq', 'dp')), may hold values from -0.0625 to 0.0625
- ffn_value_moment: float32 [7168, 2048], P(('seq', 'dp')), may hold values from -5 to 5
- ffn_value_average: float32 [7168, 2048], P(('seq', 'dp')), may hold values from -0.0625 to 0.0625
- maa_down: float32 [2048, 160], P(('seq', 'dp')), may hold values from -0.125 to 0.125
- maa_down_moment: float32 [2048, 160], P(('seq', 'dp')), may hold values from -768 to 768
- maa_down_average: float32 [2048, 160], P(('seq', 'dp')), may hold values from -0.125 to 0.125
- maa_up: float32 [5, 32, 2048], P(None, None, ('seq', 'dp')), may hold values from -0.5 to 0.5
- maa_up_moment: float32 [5, 32, 2048], P(None, None, ('seq', 'dp')), may hold values from -5 to 5
- maa_up_average: float32 [5, 32, 2048], P(None, None, ('seq', 'dp')), may hold values from -0.5 to 0.5
- decay_down: float32 [2048, 64], P(('seq', 'dp')), may hold values from -0.125 to 0.125
- decay_down_moment: float32 [2048, 64], P(('seq', 'dp')), may hold values from -5 to 5
- decay_down_average: float32 [2048, 64], P(('seq', 'dp')), may hold values from -0.125 to 0.125
- decay_up: float32 [64, 2048], P(None, ('seq', 'dp')), may hold values from -0.375 to 0.375
- decay_up_moment: float32 [64, 2048], P(None, ('seq', 'dp')), may hold values from -5 to 5
- decay_up_average: float32 [64, 2048], P(None, ('seq', 'dp')), may hold values from -0.375 to 0.375
Outputs:
- block_output: float32 [8, 1024, 2048], P('dp', 'seq')
- input_grad: float32 [8, 1024, 2048], P('dp', 'seq')
- vectors_new: float32 [16, 2048], P(None, ('seq', 'dp'))
- vectors_moment_new: float32 [16, 2048], P(None, ('seq', 'dp'))
- vectors_average_new: float32 [16, 2048], P(None, ('seq', 'dp'))
- mix_new: float32 [5, 2048, 2048], P(None, ('seq', 'dp'))
- mix_moment_new: float32 [5, 2048, 2048], P(None, ('seq', 'dp'))
- mix_average_new: float32 [5, 2048, 2048], P(None, ('seq', 'dp'))
- ffn_key_new: float32 [2048, 7168], P(('seq', 'dp'))
- ffn_key_moment_new: float32 [2048, 7168], P(('seq', 'dp'))
- ffn_key_average_new: float32 [2048, 7168], P(('seq', 'dp'))
- ffn_recept_new: float32 [2048, 2048], P(('seq', 'dp'))
- ffn_recept_moment_new: float32 [2048, 2048], P(('seq', 'dp'))
- ffn_recept_average_new: float32 [2048, 2048], P(('seq', 'dp'))
- ffn_value_new: float32 [7168, 2048], P(('seq', 'dp'))
- ffn_value_moment_new: float32 [7168, 2048], P(('seq', 'dp'))
- ffn_value_average_new: float32 [7168, 2048], P(('seq', 'dp'))
- maa_down_new: float32 [2048, 160], P(('seq', 'dp'))
- maa_down_moment_new: float32 [2048, 160], P(('seq', 'dp'))
- maa_down_average_new: float32 [2048, 160], P(('seq', 'dp'))
- maa_up_new: float32 [5, 32, 2048], P(None, None, ('seq', 'dp'))
- maa_up_moment_new: float32 [5, 32, 2048], P(None, None, ('seq', 'dp'))
- maa_up_average_new: float32 [5, 32, 2048], P(None, None, ('seq', 'dp'))
- decay_down_new: float32 [2048, 64], P(('seq', 'dp'))
- decay_down_moment_new: float32 [2048, 64], P(('seq', 'dp'))
- decay_down_average_new: float32 [2048, 64], P(('seq', 'dp'))
- decay_up_new: float32 [64, 2048], P(None, ('seq', 'dp'))
- decay_up_moment_new: float32 [64, 2048], P(None, ('seq', 'dp'))
- decay_up_average_new: float32 [64, 2048], P(None, ('seq', 'dp'))
The draws below stay inside these ranges and needn't reach their ends.
Inputs may be any that keep to these rules, and one draw needn't show every extreme that they name: `vectors`: row 8 holds negative base decays and the other rows values of order one. `lengths`: each sequence holds one document of 128 tokens and one of the rest, in either order.
All inputs are finite; a program needn't handle non-finite values.
Results may differ from the reference program's by a relative error of at most 0.0095.
The reference program's roundings to bfloat16 on the way count: a program that leaves them out, or rounds other values in their place, can miss the bound.
Values may be sent and summed in bfloat16 or wider, within the bound.
No kernel may reach another device: no remote copies, remote signals or barrier semaphores. Data moves between devices by JAX's collectives and lax.ppermute only.
A program may use at most 448 MiB of HBM per device.

```python
import math
from functools import partial
import jax
import jax.numpy as jnp
from jax import lax

FEATURE_BREADTH = 2048
FF = 7168
CHANNELS_PER_HEM = 64
MIXR = 32
DECR = 64
TOK_DEV = 256
SEG = 1024
TOKENS = 8192
N_DP = 8


def draw_lengths(key, part):
    short_len = TOK_DEV // 2
    long_len = SEG - TOK_DEV // 2
    which = jax.random.randint(jax.random.fold_in(key, 11), (N_DP,), 0, 2)
    first = jnp.where(which == 0, short_len, long_len).astype(jnp.int32)
    second = (SEG - first).astype(jnp.int32)
    return jnp.stack([first, second], axis=1).astype(jnp.int32)


def draw_vectors(key, part):
    concurrent_tracks = jax.random.split(key, 6)
    attention_heads_number = FEATURE_BREADTH // CHANNELS_PER_HEM
    scaling_settings = 1.0 + 0.1 * jax.random.normal(concurrent_tracks[0], (16, FEATURE_BREADTH), jnp.float32)
    shifting_summands = 0.2 * jax.random.normal(concurrent_tracks[1], (16, FEATURE_BREADTH), jnp.float32)
    interpolation_ratios = jax.random.uniform(concurrent_tracks[2], (16, FEATURE_BREADTH), jnp.float32)
    share = 0.5
    slow_heads = jax.random.uniform(concurrent_tracks[3], (attention_heads_number,), jnp.float32) < share
    base = jnp.where(slow_heads, jnp.log(0.5 / SEG), jnp.log(1.0 / 40.0))
    fading_items = jnp.repeat(base, CHANNELS_PER_HEM) + jax.random.uniform(concurrent_tracks[4], (FEATURE_BREADTH,), jnp.float32, -0.7, 0.7)
    present_uplift_items = 0.5 * jax.random.normal(concurrent_tracks[5], (FEATURE_BREADTH,), jnp.float32)
    aggregate_of_strip = [scaling_settings[0], shifting_summands[1], interpolation_ratios[2], interpolation_ratios[3], interpolation_ratios[4], interpolation_ratios[5], interpolation_ratios[6], interpolation_ratios[7], fading_items, present_uplift_items, scaling_settings[10], shifting_summands[11], scaling_settings[12], shifting_summands[13], interpolation_ratios[14], interpolation_ratios[15]]
    return jnp.stack(aggregate_of_strip).astype(jnp.float32)


def block_levels(stream_key, shape, pieces, low, largest):
    level = 1.0
    for axis_at, parts in pieces:
        heights = jax.random.uniform(jax.random.fold_in(jax.random.fold_in(stream_key, 6), axis_at), (parts,), jnp.float32, low / len(pieces), largest / len(pieces))
        level = level * jnp.repeat(jnp.exp(heights), shape[axis_at] // parts).reshape((-1,) + (1,) * (len(shape) - 1 - axis_at))
    return level


def scatter_about(rng, extent, deviation, limit, pieces=(), held_as=jnp.bfloat16):
    values = deviation * jax.random.normal(rng, extent, jnp.float32)
    if pieces:
        values = values * block_levels(rng, extent, pieces, -0.22, 0.18)
    return jnp.clip(values, -limit, limit).astype(held_as)


def setup_inputs(seed: int = 0) -> dict:
    key_of = jax.random.split(jax.random.key(seed), 31)
    block_input = scatter_about(key_of[0], (N_DP, SEG, FEATURE_BREADTH), 1.0, 6.0, ((0, 8), (1, 4)))
    out_grad = scatter_about(key_of[1], (N_DP, SEG, FEATURE_BREADTH), 1.0, 6.0, ((0, 8), (1, 4)))
    lengths = draw_lengths(jax.random.fold_in(key_of[30], 71), 0)
    vectors = draw_vectors(jax.random.fold_in(key_of[30], 71), 0)
    vectors_moment = scatter_about(key_of[4], (16, FEATURE_BREADTH), (0.05 * TOKENS ** 0.5), 28.0, ((1, 32),), jnp.float32)
    vectors_average = scatter_about(key_of[5], (16, FEATURE_BREADTH), 0.5, 3.0, ((1, 32),), jnp.float32)
    mix_weights = scatter_about(key_of[6], (5, FEATURE_BREADTH, FEATURE_BREADTH), FEATURE_BREADTH ** -0.5, 0.125, ((1, 32),), jnp.float32)
    mix_moment = scatter_about(key_of[7], (5, FEATURE_BREADTH, FEATURE_BREADTH), (0.01 * TOKENS ** 0.5), 5.0, ((1, 32),), jnp.float32)
    mix_average = scatter_about(key_of[8], (5, FEATURE_BREADTH, FEATURE_BREADTH), FEATURE_BREADTH ** -0.5, 0.125, ((1, 32),), jnp.float32)
    ffn_key = scatter_about(key_of[9], (FEATURE_BREADTH, FF), FEATURE_BREADTH ** -0.5, 0.125, ((0, 32),), jnp.float32)
    ffn_key_moment = scatter_about(key_of[10], (FEATURE_BREADTH, FF), (0.01 * TOKENS ** 0.5), 5.0, ((0, 32),), jnp.float32)
    ffn_key_average = scatter_about(key_of[11], (FEATURE_BREADTH, FF), FEATURE_BREADTH ** -0.5, 0.125, ((0, 32),), jnp.float32)
    ffn_recept = scatter_about(key_of[12], (FEATURE_BREADTH, FEATURE_BREADTH), FEATURE_BREADTH ** -0.5, 0.125, ((0, 32),), jnp.float32)
    ffn_recept_moment = scatter_about(key_of[13], (FEATURE_BREADTH, FEATURE_BREADTH), (0.01 * TOKENS ** 0.5), 5.0, ((0, 32),), jnp.float32)
    ffn_recept_average = scatter_about(key_of[14], (FEATURE_BREADTH, FEATURE_BREADTH), FEATURE_BREADTH ** -0.5, 0.125, ((0, 32),), jnp.float32)
    ffn_value = scatter_about(key_of[15], (FF, FEATURE_BREADTH), FF ** -0.5, 0.0625, ((0, 32),), jnp.float32)
    ffn_value_moment = scatter_about(key_of[16], (FF, FEATURE_BREADTH), (0.01 * TOKENS ** 0.5), 5.0, ((0, 32),), jnp.float32)
    ffn_value_average = scatter_about(key_of[17], (FF, FEATURE_BREADTH), FF ** -0.5, 0.0625, ((0, 32),), jnp.float32)
    maa_down = scatter_about(key_of[18], (FEATURE_BREADTH, 5 * MIXR), FEATURE_BREADTH ** -0.5, 0.125, ((0, 32),), jnp.float32)
    maa_down_moment = scatter_about(key_of[19], (FEATURE_BREADTH, 5 * MIXR), (1.5 * TOKENS ** 0.5), 768.0, ((0, 32),), jnp.float32)
    maa_down_average = scatter_about(key_of[20], (FEATURE_BREADTH, 5 * MIXR), FEATURE_BREADTH ** -0.5, 0.125, ((0, 32),), jnp.float32)
    maa_up = scatter_about(key_of[21], (5, MIXR, FEATURE_BREADTH), (0.5 * MIXR ** -0.5), 0.5, ((2, 32),), jnp.float32)
    maa_up_moment = scatter_about(key_of[22], (5, MIXR, FEATURE_BREADTH), (0.01 * TOKENS ** 0.5), 5.0, ((2, 32),), jnp.float32)
    maa_up_average = scatter_about(key_of[23], (5, MIXR, FEATURE_BREADTH), (0.5 * MIXR ** -0.5), 0.5, ((2, 32),), jnp.float32)
    decay_down = scatter_about(key_of[24], (FEATURE_BREADTH, DECR), FEATURE_BREADTH ** -0.5, 0.125, ((0, 32),), jnp.float32)
    decay_down_moment = scatter_about(key_of[25], (FEATURE_BREADTH, DECR), (0.01 * TOKENS ** 0.5), 5.0, ((0, 32),), jnp.float32)
    decay_down_average = scatter_about(key_of[26], (FEATURE_BREADTH, DECR), FEATURE_BREADTH ** -0.5, 0.125, ((0, 32),), jnp.float32)
    decay_up = scatter_about(key_of[27], (DECR, FEATURE_BREADTH), (0.5 * DECR ** -0.5), 0.375, ((1, 32),), jnp.float32)
    decay_up_moment = scatter_about(key_of[28], (DECR, FEATURE_BREADTH), (0.01 * TOKENS ** 0.5), 5.0, ((1, 32),), jnp.float32)
    decay_up_average = scatter_about(key_of[29], (DECR, FEATURE_BREADTH), (0.5 * DECR ** -0.5), 0.375, ((1, 32),), jnp.float32)
    return {"block_input": block_input, "out_grad": out_grad, "lengths": lengths, "vectors": vectors, "vectors_moment": vectors_moment, "vectors_average": vectors_average, "mix_weights": mix_weights, "mix_moment": mix_moment, "mix_average": mix_average, "ffn_key": ffn_key, "ffn_key_moment": ffn_key_moment, "ffn_key_average": ffn_key_average, "ffn_recept": ffn_recept, "ffn_recept_moment": ffn_recept_moment, "ffn_recept_average": ffn_recept_average, "ffn_value": ffn_value, "ffn_value_moment": ffn_value_moment, "ffn_value_average": ffn_value_average, "maa_down": maa_down, "maa_down_moment": maa_down_moment, "maa_down_average": maa_down_average, "maa_up": maa_up, "maa_up_moment": maa_up_moment, "maa_up_average": maa_up_average, "decay_down": decay_down, "decay_down_moment": decay_down_moment, "decay_down_average": decay_down_average, "decay_up": decay_up, "decay_up_moment": decay_up_moment, "decay_up_average": decay_up_average}


@jax.custom_vjp
def low(v):
    return lax.optimization_barrier(v.astype(jnp.bfloat16)).astype(jnp.float32)

@jax.custom_vjp
def low_back(v):
    return v

def low_keep(v):
    return (low(v), None)

def low_pass(kept, grad):
    return (grad,)

def back_keep(v):
    return (v, None)

def back_low(kept, grad):
    return (low(grad),)
low.defvjp(low_keep, low_pass)
low_back.defvjp(back_keep, back_low)
highest_precision = lax.Precision.HIGHEST
factors = (0.2, 0.03, 0.03, 0.03, 0.03, 0.03, 0.03, 0.03, 0.03)

def layer_norm(field, gain, bias):
    center = field - lax.optimization_barrier(jnp.mean(field, axis=-1, keepdims=True))
    spread = lax.optimization_barrier(jnp.mean(center * center, axis=-1, keepdims=True))
    return center * lax.rsqrt(spread + 1e-05) * gain + bias

def norm_first(field, blending_arrays):
    return layer_norm(field, blending_arrays[0], blending_arrays[1])

def norm_second(field, blending_arrays):
    return layer_norm(field, blending_arrays[12], blending_arrays[13])

def gate_part(raw_output, gate, blending_arrays):
    center = raw_output - lax.optimization_barrier(jnp.mean(raw_output, axis=-1, keepdims=True))
    spread = lax.optimization_barrier(jnp.mean(center * center, axis=-1, keepdims=True))
    normal_draw = (center * lax.rsqrt(spread + 0.00064)).reshape(gate.shape)
    return (normal_draw * blending_arrays[10] + blending_arrays[11]) * jax.nn.silu(gate)

def mix_inputs(normed, incoming, blending_arrays, mix_down_weight, mix_up_weight, ddown, dup, follows):
    local_tokens = normed.shape[0]
    prior = jnp.concatenate([incoming, normed[:-1]], axis=0) * follows[:, None]
    delta = prior - normed
    mixed_input = normed + delta * blending_arrays[2]
    low_rank_adapter = jnp.tanh(jnp.dot(mixed_input, mix_down_weight, precision=highest_precision)).reshape(local_tokens, 5, mix_up_weight.shape[1])
    start_offsets = jnp.einsum('vjs,jsz->vjz', low_rank_adapter, mix_up_weight, precision=highest_precision)
    inputs = normed[:, None] + delta[:, None] * (blending_arrays[3:8][None] + start_offsets)
    decay = blending_arrays[8] + jnp.dot(jnp.tanh(jnp.dot(inputs[:, 0], ddown, precision=highest_precision)), dup, precision=highest_precision)
    return (inputs[:, 1], inputs[:, 2], inputs[:, 3], inputs[:, 4], -jnp.exp(decay))

def channel_inputs(second, incoming, blending_arrays, follows):
    prior = jnp.concatenate([incoming, second[:-1]], axis=0) * follows[:, None]
    delta = prior - second
    return (second + delta * blending_arrays[14], second + delta * blending_arrays[15])

def recursive_section(current_boost_param, memory_table, segment_parts):
    acceptance_lines, lookup_lines, payload_lines, logarithmic_forgetting, segment_groups, prior = segment_parts
    order = jnp.arange(acceptance_lines.shape[0])
    total = jnp.cumsum(logarithmic_forgetting, axis=0)
    before = total - logarithmic_forgetting
    lower = (order[:, None] > order[None, :]) & (segment_groups[:, None] == segment_groups[None, :])
    lower_f = lower.astype(jnp.float32)[:, :, None, None]
    gap = jnp.where(lower[:, :, None, None], before[:, None] - total[None, :], 0.0)
    scores = jnp.einsum('thk,shk,tshk->tsh', acceptance_lines, lookup_lines, jnp.exp(gap) * lower_f, precision=highest_precision)
    diagonal_contribution = lax.optimization_barrier(jnp.sum(acceptance_lines * current_boost_param[None] * lookup_lines, axis=-1))
    stratum_result = jnp.einsum('tsh,shv->thv', scores, payload_lines, precision=highest_precision) + diagonal_contribution[:, :, None] * payload_lines
    carried = (segment_groups == prior).astype(jnp.float32)
    query_rows = acceptance_lines * jnp.exp(before) * carried[:, None, None]
    stratum_result = stratum_result + jnp.einsum('yco,cor->ycr', query_rows, memory_table, precision=highest_precision)
    last = total[-1]
    keep = (segment_groups[-1] == prior).astype(jnp.float32)
    live = (segment_groups == segment_groups[-1]).astype(jnp.float32)
    weighted_sum = lookup_lines * jnp.exp(last[None] - total) * live[:, None, None]
    fresh_state = jnp.einsum('dcm,dcy->cmy', weighted_sum, payload_lines, precision=highest_precision)
    memory_table = memory_table * (jnp.exp(last) * keep)[:, :, None] + fresh_state
    return (memory_table, stratum_result)

def partitioned_recursion(acceptance_lines, lookup_lines, payload_lines, logarithmic_forgetting, current_boost_param, segment_groups, preceding_segment):
    length, attention_heads_number, embedding_extent = acceptance_lines.shape
    blocks = length // 32
    doc_blocks = segment_groups.reshape(blocks, 32)
    priors = jnp.concatenate([jnp.reshape(preceding_segment, (1,)).astype(jnp.int32), doc_blocks[:-1, -1].astype(jnp.int32)])
    opening_memory = jnp.zeros((attention_heads_number, embedding_extent, embedding_extent), jnp.float32)
    segment_parts = (acceptance_lines.reshape(blocks, 32, attention_heads_number, embedding_extent), lookup_lines.reshape(blocks, 32, attention_heads_number, embedding_extent), payload_lines.reshape(blocks, 32, attention_heads_number, embedding_extent), logarithmic_forgetting.reshape(blocks, 32, attention_heads_number, embedding_extent), doc_blocks, priors)
    closing_memory, stratum_result = lax.scan(jax.checkpoint(partial(recursive_section, current_boost_param)), opening_memory, segment_parts)
    return (stratum_result.reshape(length, attention_heads_number, embedding_extent), closing_memory)

def matmul(left_factor, right_factor):
    return jnp.einsum('gcw,wo->gco', left_factor, right_factor, precision=highest_precision)

def forward(hidden, blending_arrays, mix, fkey, frec, fval, mix_down_weight, mix_up_weight, ddown, dup, segment_groups=None, follows=None):
    seqs, length, embedding_extent = hidden.shape
    attention_heads_number = embedding_extent // CHANNELS_PER_HEM
    blank = jnp.zeros((seqs, 1, embedding_extent), jnp.float32)
    normed = norm_first(hidden, blending_arrays)
    mapped = jax.vmap(mix_inputs, in_axes=(0, 0, None, None, None, None, None, 0))
    xkey, xval, xrec, xgate, logarithmic_forgetting = mapped(normed, blank, blending_arrays, mix_down_weight, mix_up_weight, ddown, dup, follows)
    lookup_lines = low_back(matmul(low(xkey), low(mix[0])))
    payload_lines = low_back(matmul(low(xval), low(mix[1])))
    acceptance_lines = low_back(matmul(low(xrec), low(mix[2])))
    gate = low_back(matmul(low(xgate), low(mix[3])))
    current_boost_param = blending_arrays[9].reshape(attention_heads_number, CHANNELS_PER_HEM)

    def one_sequence(segment_parts):
        solo_acceptance, solo_lookup, solo_payload, solo_forgetting, solo_segment = segment_parts
        return partitioned_recursion(solo_acceptance, solo_lookup, solo_payload, solo_forgetting, current_boost_param, solo_segment, jnp.array(-1, jnp.int32))[0]
    split_shape = (seqs, length, attention_heads_number, CHANNELS_PER_HEM)
    raw_output = lax.map(one_sequence, (acceptance_lines.reshape(split_shape), lookup_lines.reshape(split_shape), payload_lines.reshape(split_shape), logarithmic_forgetting.reshape(split_shape), segment_groups))
    gated = gate_part(raw_output, gate, blending_arrays)
    attn = low_back(matmul(low(gated), low(mix[4])))
    middle = hidden + attn
    second = norm_second(middle, blending_arrays)
    key_in, rec_in = jax.vmap(channel_inputs, in_axes=(0, 0, None, 0))(second, blank, blending_arrays, follows)
    kpre = low_back(matmul(low(key_in), low(fkey)))
    squared = jnp.square(jax.nn.relu(kpre))
    kvals = low_back(matmul(low(squared), low(fval)))
    rpre = low_back(matmul(low(rec_in), low(frec)))
    return middle + jax.nn.sigmoid(rpre) * kvals

def renew(weight, moment, average, grad, factor):
    rate = factor / math.sqrt(TOKENS)
    moment = 0.9 * moment + grad
    weight = weight - rate * (grad + 0.9 * moment)
    average = 0.8 * average + 0.2 * weight
    return (weight, moment, average)

def reference(block_input, out_grad, lengths, vectors, vectors_moment, vectors_average, mix_weights, mix_moment, mix_average, ffn_key, ffn_key_moment, ffn_key_average, ffn_recept, ffn_recept_moment, ffn_recept_average, ffn_value, ffn_value_moment, ffn_value_average, maa_down, maa_down_moment, maa_down_average, maa_up, maa_up_moment, maa_up_average, decay_down, decay_down_moment, decay_down_average, decay_up, decay_up_moment, decay_up_average):
    hidden = block_input.astype(jnp.float32)
    segment_groups = (jnp.arange(SEG)[None, :] >= lengths[:, :1]).astype(jnp.int32)
    previous = jnp.concatenate([jnp.full((segment_groups.shape[0], 1), -1, jnp.int32), segment_groups[:, :-1]], axis=1)
    follows = (segment_groups == previous).astype(jnp.float32)
    params = (vectors, mix_weights, ffn_key, ffn_recept, ffn_value, maa_down, maa_up, decay_down, decay_up)
    moments = (vectors_moment, mix_moment, ffn_key_moment, ffn_recept_moment, ffn_value_moment, maa_down_moment, maa_up_moment, decay_down_moment, decay_up_moment)
    averages = (vectors_average, mix_average, ffn_key_average, ffn_recept_average, ffn_value_average, maa_down_average, maa_up_average, decay_down_average, decay_up_average)
    stratum_result, pull = jax.vjp(partial(forward, segment_groups=segment_groups, follows=follows), hidden, *params)
    grads = pull(out_grad.astype(jnp.float32))
    results = [stratum_result, grads[0]]
    for index in range(9):
        results.extend(renew(params[index], moments[index], averages[index], grads[index + 1], factors[index]))
    return tuple(results)
```

```python
import functools
import math

import jax
import jax.numpy as jnp
import numpy as np
from jax import lax
from jax.experimental import pallas as pl
from jax.experimental.pallas import tpu as pltpu
from jax.sharding import PartitionSpec as P

HEAD = 64
LANES = 128
CHUNK = 64
BF = jnp.bfloat16
F32 = jnp.float32
NN = (((1,), (0,)), ((), ()))
NT = (((1,), (1,)), ((), ()))
TN = (((0,), (0,)), ((), ()))


def levels_of(chunk):
    return [1 << e for e in reversed(range(chunk.bit_length() - 1))]


def tables(chunk):
    levels = levels_of(chunk)
    at = np.arange(chunk)
    sums = []
    for m in levels[:-1]:
        same = at[:, None] // (2 * m) == at[None, :] // (2 * m)
        right = (at & m) > 0
        up = same & right[:, None] & right[None, :] & (at[None, :] < at[:, None])
        down = same & ~right[:, None] & ~right[None, :] & (at[None, :] > at[:, None])
        sums.append(up | down)
    sums.append(at[None, :] < at[:, None])
    sums.append(at[None, :] > at[:, None])
    sums = np.concatenate(sums, 0).astype(np.float32)
    level = np.full((chunk, chunk), -1, np.int32)
    for index, m in enumerate(levels):
        same = at[:, None] // (2 * m) == at[None, :] // (2 * m)
        right = (at & m) > 0
        level = np.where(same & (right[:, None] != right[None, :]), index, level)
    level = np.concatenate([level, level], 1)
    ones = (np.arange(LANES)[:, None] // HEAD == np.arange(LANES)[None, :] // HEAD).astype(np.float32)
    return sums, level, ones


def split(value, parts):
    pieces = []
    for _ in range(parts):
        piece = value.astype(BF)
        pieces.append(piece)
        value = value - piece.astype(F32)
    return pieces


def dot3(left, right, dims):
    lh, ll = left
    rh, rl = right
    la, ra = dims[0][0][0], dims[0][1][0]
    return lax.dot_general(
        jnp.concatenate([lh, lh, ll], la),
        jnp.concatenate([rh, rl, rh], ra),
        dims,
        preferred_element_type=F32,
    )


def two(value):
    return split(value, 2)


def spread(pieces, heads):
    return [jnp.where(heads, jnp.concatenate([p, p], 0), jnp.zeros((), p.dtype)) for p in pieces]


def exponents(sums_ref, ld, lo, hi):
    parts = jnp.concatenate(split(ld, 3), 0)
    c = sums_ref[lo:hi, :]
    return lax.dot_general(
        jnp.concatenate([c, c, c], 1), parts, NN, preferred_element_type=F32
    )


def head_mask(rows):
    r = lax.broadcasted_iota(jnp.int32, (2 * rows, LANES), 0) >= rows
    c = lax.broadcasted_iota(jnp.int32, (2 * rows, LANES), 1) >= HEAD
    return r == c


def head_sum(value, ones_ref):
    a, b = two(value)
    return lax.dot_general(
        jnp.concatenate([a, b], 1),
        jnp.concatenate([ones_ref[...], ones_ref[...]], 0),
        NN,
        preferred_element_type=F32,
    )


def silu(x):
    return x / (1.0 + jnp.exp(-x))


def close_kernel(keep_ref, k_ref, v_ref, ld_ref, sums_ref, state_ref, carry_ref):
    tokens = k_ref.shape[0]
    heads = head_mask(HEAD)
    state = jnp.zeros((LANES, LANES), F32)
    carry = jnp.ones((1, LANES), F32)
    n = sums_ref.shape[0] // CHUNK
    for c in range(tokens // CHUNK):
        rows = pl.ds(c * CHUNK, CHUNK)
        keep = keep_ref[c]
        ld = ld_ref[rows, :]
        e = exponents(sums_ref, ld, (n - 1) * CHUNK, n * CHUNK)
        last = jnp.exp(e[0:1] + ld[0:1]) * keep
        carry = carry * last
        fresh = dot3(two(v_ref[rows, :]), two(k_ref[rows, :] * jnp.exp(e)), TN)
        state = state * last + jnp.where(heads, fresh, 0.0)
    state_ref[...] = state[:HEAD] + state[HEAD:]
    carry_ref[...] = carry


def level_part(index, m, q, k, x):
    right = (lax.broadcasted_iota(jnp.int32, (CHUNK, LANES), 0) & m) > 0
    z = jnp.where(right, q, k)
    if m > 1:
        z = z * x[index * CHUNK : (index + 1) * CHUNK]
    return right, z


def forward_kernel(
    keep_ref, q_ref, k_ref, v_ref, ld_ref, gate_ref, vec_ref, start_ref, sums_ref, level_ref, ones_ref,
    raw_ref, gated_ref, score_ref, state_ref,
):
    tokens = q_ref.shape[0]
    levels = levels_of(CHUNK)
    n = sums_ref.shape[0] // CHUNK
    heads = head_mask(HEAD)
    wide = head_mask(CHUNK)
    level = level_ref[...]
    t = lax.broadcasted_iota(jnp.int32, (CHUNK, 2 * CHUNK), 0)
    s = lax.broadcasted_iota(jnp.int32, (CHUNK, 2 * CHUNK), 1) & (CHUNK - 1)
    bonus = vec_ref[0:1]
    state = jnp.where(heads, jnp.concatenate([start_ref[...], start_ref[...]], 0), 0.0)
    for c in range(tokens // CHUNK):
        rows = pl.ds(c * CHUNK, CHUNK)
        state = state * keep_ref[c]
        state_ref[pl.ds(c * HEAD, HEAD), :] = state[:HEAD] + state[HEAD:]
        q, k, v, ld = q_ref[rows, :], k_ref[rows, :], v_ref[rows, :], ld_ref[rows, :]
        e = exponents(sums_ref, ld, 0, n * CHUNK)
        x = jnp.exp(e)
        score = jnp.zeros((CHUNK, 2 * CHUNK), F32)
        for index, m in enumerate(levels):
            right, z = level_part(index, m, q, k, x)
            z = two(z)
            score = jnp.where(level == index, dot3(z, spread(z, wide), NT), score)
        score = jnp.where(t > s, score, 0.0)
        score = jnp.where(t == s, head_sum(q * bonus * k, ones_ref), score)
        score_ref[rows, :] = score
        xq, xk = x[(n - 2) * CHUNK : (n - 1) * CHUNK], x[(n - 1) * CHUNK :]
        v2 = two(v)
        raw = dot3(two(score), spread(v2, wide), NN) + dot3(two(q * xq), two(state), NT)
        last = jnp.exp(e[(n - 1) * CHUNK : (n - 1) * CHUNK + 1] + ld[0:1])
        state = state * last + jnp.where(heads, dot3(v2, two(k * xk), TN), 0.0)
        raw_ref[rows, :] = raw
        center = raw - head_sum(raw, ones_ref) * (1.0 / HEAD)
        spread_of = head_sum(center * center, ones_ref) * (1.0 / HEAD)
        normal = center * lax.rsqrt(spread_of + 0.00064)
        gated_ref[rows, :] = ((normal * vec_ref[1:2] + vec_ref[2:3]) * silu(gate_ref[rows, :])).astype(BF)


def head_back_kernel(
    keep_ref, q_ref, ld_ref, raw_ref, gate_ref, grad_ref, vec_ref, sums_ref, ones_ref,
    draw_ref, dgate_ref, direct_ref, dvec_ref,
):
    tokens = q_ref.shape[0]
    n = sums_ref.shape[0] // CHUNK
    heads = head_mask(HEAD)
    direct = jnp.zeros((LANES, LANES), F32)
    gain, bias = vec_ref[1:2], vec_ref[2:3]
    dgain = jnp.zeros((1, LANES), F32)
    dbias = jnp.zeros((1, LANES), F32)
    for c in reversed(range(tokens // CHUNK)):
        rows = pl.ds(c * CHUNK, CHUNK)
        raw, gate, grad = raw_ref[rows, :], gate_ref[rows, :], grad_ref[rows, :]
        center = raw - head_sum(raw, ones_ref) * (1.0 / HEAD)
        inv = lax.rsqrt(head_sum(center * center, ones_ref) * (1.0 / HEAD) + 0.00064)
        normal = center * inv
        sig = 1.0 / (1.0 + jnp.exp(-gate))
        act = gate * sig
        affine = normal * gain + bias
        dgate_ref[rows, :] = (grad * affine * (sig + act * (1.0 - sig))).astype(BF)
        daff = grad * act
        dgain = dgain + jnp.sum(daff * normal, 0, keepdims=True)
        dbias = dbias + jnp.sum(daff, 0, keepdims=True)
        dnorm = daff * gain
        draw = inv * (
            dnorm
            - head_sum(dnorm, ones_ref) * (1.0 / HEAD)
            - normal * (head_sum(dnorm * normal, ones_ref) * (1.0 / HEAD))
        )
        draw_ref[rows, :] = draw
        ld = ld_ref[rows, :]
        e = exponents(sums_ref, ld, (n - 2) * CHUNK, (n - 1) * CHUNK)
        last = jnp.exp(e[CHUNK - 1 :] + ld[CHUNK - 1 :])
        fresh = dot3(two(draw), two(q_ref[rows, :] * jnp.exp(e)), TN)
        direct = (direct * last + jnp.where(heads, fresh, 0.0)) * keep_ref[c]
    direct_ref[...] = direct[:HEAD] + direct[HEAD:]
    dvec_ref[0:1] = dgain
    dvec_ref[1:2] = dbias


def backward_kernel(
    keep_ref, q_ref, k_ref, v_ref, ld_ref, draw_ref, score_ref, state_ref, later_ref, vec_ref,
    sums_ref, sums_t_ref, level_ref, ones_ref,
    dq_ref, dk_ref, dv_ref, dld_ref, du_ref,
):
    tokens = q_ref.shape[0]
    levels = levels_of(CHUNK)
    n = sums_ref.shape[0] // CHUNK
    heads = head_mask(HEAD)
    wide = head_mask(CHUNK)
    level = level_ref[...]
    t = lax.broadcasted_iota(jnp.int32, (CHUNK, 2 * CHUNK), 0)
    s = lax.broadcasted_iota(jnp.int32, (CHUNK, 2 * CHUNK), 1) & (CHUNK - 1)
    lower = t > s
    bonus = vec_ref[0:1]
    dstate = jnp.where(heads, jnp.concatenate([later_ref[...], later_ref[...]], 0), 0.0)
    du = jnp.zeros((1, LANES), F32)
    for c in reversed(range(tokens // CHUNK)):
        rows = pl.ds(c * CHUNK, CHUNK)
        small = state_ref[pl.ds(c * HEAD, HEAD), :]
        state = jnp.where(heads, jnp.concatenate([small, small], 0), 0.0)
        q, k, v, ld = q_ref[rows, :], k_ref[rows, :], v_ref[rows, :], ld_ref[rows, :]
        draw = draw_ref[rows, :]
        e = exponents(sums_ref, ld, 0, n * CHUNK)
        x = jnp.exp(e)
        v2, draw2 = two(v), two(draw)
        dscore = jnp.where(
            lower, dot3(draw2, spread(v2, wide), NT), dot3(v2, spread(draw2, wide), NT)
        )
        dbon = head_sum(draw * v, ones_ref) * bonus
        dq = dbon * k
        dk = dbon * q
        du = du + jnp.sum(head_sum(draw * v, ones_ref) * q * k, 0, keepdims=True)
        grads = []
        for index, m in enumerate(levels):
            right, z = level_part(index, m, q, k, x)
            dz = dot3(
                two(jnp.where(level == index, dscore, 0.0)), spread(two(z), wide), NN
            )
            if m > 1:
                grads.append(z * dz)
                dz = dz * x[index * CHUNK : (index + 1) * CHUNK]
            dq = dq + jnp.where(right, dz, 0.0)
            dk = dk + jnp.where(right, 0.0, dz)
        xq, xk = x[(n - 2) * CHUNK : (n - 1) * CHUNK], x[(n - 1) * CHUNK :]
        qx, kx = q * xq, k * xk
        dstate2 = two(dstate)
        dqx = dot3(draw2, two(state), NN)
        dkx = dot3(v2, dstate2, NN)
        grads.append(dqx * qx)
        grads.append(dkx * kx)
        dq_ref[rows, :] = (dq + dqx * xq).astype(dq_ref.dtype)
        dk_ref[rows, :] = (dk + dkx * xk).astype(dk_ref.dtype)
        back = dot3(two(score_ref[rows, :]), draw2, TN)
        back = jnp.where(wide, back, 0.0)
        dv_ref[rows, :] = (back[:CHUNK] + back[CHUNK:] + dot3(two(kx), dstate2, NT)).astype(dv_ref.dtype)
        last = jnp.exp(e[(n - 1) * CHUNK : (n - 1) * CHUNK + 1] + ld[0:1])
        through = jnp.sum(state * dstate, 0, keepdims=True) * last
        gh, gl = two(jnp.concatenate(grads, 0))
        ct = sums_t_ref[...]
        dld_ref[rows, :] = through + lax.dot_general(
            jnp.concatenate([ct, ct], 1), jnp.concatenate([gh, gl], 0), NN, preferred_element_type=F32
        )
        dstate = dstate * last + jnp.where(heads, dot3(draw2, two(qx), TN), 0.0)
        dstate = dstate * keep_ref[c]
    du_ref[...] = du


def _call(kernel, outs, ins, tokens, width, flops):
    def spec(kind):
        kind, rows = kind
        if kind == "s":
            return pl.BlockSpec(memory_space=pltpu.SMEM)
        if kind == "c":
            return pl.BlockSpec(rows, lambda i: (0, 0))
        return pl.BlockSpec((rows, LANES), lambda i: (0, i))

    return pl.pallas_call(
        kernel,
        grid=(width // LANES,),
        in_specs=[spec(kind) for kind, _ in ins],
        out_specs=[spec(("r", rows)) for rows, _ in outs],
        out_shape=[jax.ShapeDtypeStruct((rows, width), dt) for rows, dt in outs],
        compiler_params=pltpu.CompilerParams(vmem_limit_bytes=48 * 2**20),
        cost_estimate=pl.CostEstimate(flops=flops, bytes_accessed=10 * tokens * width * 4, transcendentals=8 * tokens * width),
    )(*[value for _, value in ins])


def rows_of(value):
    return (("r", value.shape[0]), value)


def const_of(value):
    return (("c", value.shape), value)


def close(keep, k, v, ld):
    tokens, width = k.shape
    sums, _, _ = tables(CHUNK)
    return _call(
        close_kernel, [(HEAD, F32), (1, F32)],
        [(("s", 0), keep), rows_of(k), rows_of(v), rows_of(ld), const_of(jnp.asarray(sums, BF))],
        tokens, width, tokens * width * 2000,
    )


def forward(keep, q, k, v, ld, gate, vec3, start):
    tokens, width = k.shape
    sums, level, ones = tables(CHUNK)
    return _call(
        forward_kernel,
        [(tokens, F32), (tokens, BF), (tokens, F32), (tokens // CHUNK * HEAD, F32)],
        [(("s", 0), keep), rows_of(q), rows_of(k), rows_of(v), rows_of(ld), rows_of(gate), rows_of(vec3), rows_of(start),
         const_of(jnp.asarray(sums, BF)), const_of(jnp.asarray(level)), const_of(jnp.asarray(ones, BF))],
        tokens, width, tokens * width * 20000,
    )


def head_back(keep, q, ld, raw, gate, grad, vec3):
    tokens, width = q.shape
    sums, level, ones = tables(CHUNK)
    return _call(
        head_back_kernel,
        [(tokens, F32), (tokens, BF), (HEAD, F32), (2, F32)],
        [(("s", 0), keep), rows_of(q), rows_of(ld), rows_of(raw), rows_of(gate), rows_of(grad), rows_of(vec3),
         const_of(jnp.asarray(sums, BF)), const_of(jnp.asarray(ones, BF))],
        tokens, width, tokens * width * 4000,
    )


def backward(keep, q, k, v, ld, draw, score, state, later, vec3):
    tokens, width = q.shape
    sums, level, ones = tables(CHUNK)
    return _call(
        backward_kernel,
        [(tokens, BF), (tokens, BF), (tokens, BF), (tokens, F32), (1, F32)],
        [(("s", 0), keep), rows_of(q), rows_of(k), rows_of(v), rows_of(ld), rows_of(draw), rows_of(score), rows_of(state),
         rows_of(later), rows_of(vec3), const_of(jnp.asarray(sums, BF)), const_of(jnp.asarray(sums.T.copy(), BF)),
         const_of(jnp.asarray(level)), const_of(jnp.asarray(ones, BF))],
        tokens, width, tokens * width * 30000,
    )


HIGHEST = lax.Precision.HIGHEST
FACTORS = (0.2, 0.03, 0.03, 0.03, 0.03, 0.03, 0.03, 0.03, 0.03)
BOTH = ("seq", "dp")


def layer_norm(field, gain, bias):
    center = field - jnp.mean(field, axis=-1, keepdims=True)
    spread_of = jnp.mean(center * center, axis=-1, keepdims=True)
    return center * lax.rsqrt(spread_of + 1e-05) * gain + bias


def norm_first(field, vecs):
    return layer_norm(field, vecs[0], vecs[1])


def norm_second(field, vecs):
    return layer_norm(field, vecs[12], vecs[13])


def shifted(field, incoming, follows):
    return jnp.concatenate([incoming, field[:-1]], axis=0) * follows


def mix_inputs(normed, incoming, vecs, down, up, ddown, dup, follows):
    delta = shifted(normed, incoming, follows) - normed
    lora = jnp.tanh(jnp.dot(normed + delta * vecs[2], down, precision=HIGHEST))
    rank = lora.shape[1] // 5
    inputs = [
        normed
        + delta
        * (
            vecs[3 + c]
            + jnp.dot(
                lora[:, c * rank : (c + 1) * rank], up[c * rank : (c + 1) * rank], precision=HIGHEST
            )
        )
        for c in range(5)
    ]
    decay = vecs[8] + jnp.dot(
        jnp.tanh(jnp.dot(inputs[0], ddown, precision=HIGHEST)), dup, precision=HIGHEST
    )
    return (inputs[1], inputs[2], inputs[3], inputs[4], -jnp.exp(decay))


def channel_inputs(second, incoming, vecs, follows):
    delta = shifted(second, incoming, follows) - second
    return (second + delta * vecs[14], second + delta * vecs[15])


def send_rows(field):
    n = lax.axis_size("seq")
    return lax.ppermute(field[-1:], "seq", [(i, i + 1) for i in range(n - 1)])


def back_rows(grad_first, field):
    n = lax.axis_size("seq")
    arrived = lax.ppermute(grad_first, "seq", [(i + 1, i) for i in range(n - 1)])
    last = lax.broadcasted_iota(jnp.int32, field.shape, 0) == field.shape[0] - 1
    return field + jnp.where(last, arrived, 0.0)


def prefix(carry, state, reverse):
    n, here = lax.axis_size("seq"), lax.axis_index("seq")
    every = lax.all_gather(jnp.concatenate([state, carry], 0), "seq")
    total = jnp.zeros_like(state)
    for k in range(n):
        at = n - 1 - k if reverse else k
        reached = at > here if reverse else at < here
        total = jnp.where(reached, every[at, -1:] * total + every[at, :-1], total)
    return total


def product(left, right):
    return jnp.dot(left, right, preferred_element_type=F32)


def product_t(left, right):
    return lax.dot_general(left, right, TN, preferred_element_type=F32)


def back_product(grad, weight):
    return lax.dot_general(grad, weight, NT, preferred_element_type=F32)


def swap(value, axis, bit):
    return lax.ppermute(value, axis, [(i, i ^ bit) for i in range(lax.axis_size(axis))])


def climb(value, step, count):
    planes = lax.axis_size("dp") // 2
    pairs = []
    for z in range(planes):
        if (step > 0 and z < count and z + 1 < planes) or (step < 0 and z >= planes - count and z > 0):
            pairs += [(2 * z + y, 2 * (z + step) + y) for y in (0, 1)]
    return lax.ppermute(value, "dp", pairs)


def pick(value, index, axis=0):
    return lax.dynamic_index_in_dim(value, index, axis, keepdims=False)


def down_z(whole, kind):
    z = lax.axis_index("dp") // 2
    planes = whole.shape[0]
    ends = []
    for step in (1, -1):
        carried = None
        for t in range(1, planes):
            part = pick(whole, (z + step * (planes - t)) % planes)
            carried = part if carried is None else part + carried
            carried = climb(carried.astype(kind), step, t).astype(F32)
        ends.append(carried)
    return pick(whole, z) + ends[0] + ends[1]


def scatter_sum(block, rows, kind, x_first):
    s, d = lax.axis_index("seq"), lax.axis_index("dp")
    y = d % 2

    def parts(value):
        return value.reshape(4, 2, rows, value.shape[-1])

    far = swap(block(s ^ 3).astype(kind), "seq", 1)
    near = swap(block(s ^ 1).astype(kind), "seq", 1)
    if x_first:
        across = swap((block(s ^ 2) + far.astype(F32)).astype(kind), "seq", 2)
        own = parts(block(s) + near.astype(F32) + across.astype(F32))
        other = swap(pick(own, 1 - y, 1).astype(kind), "dp", 1)
        own = pick(own, y, 1) + other.astype(F32)
    else:
        across = parts(block(s ^ 2) + far.astype(F32))
        own = parts(block(s) + near.astype(F32))
        a = swap(pick(across, 1 - y, 1).astype(kind), "dp", 1)
        b = swap(pick(own, 1 - y, 1).astype(kind), "dp", 1)
        a = swap((pick(across, y, 1) + a.astype(F32)).astype(kind), "seq", 2)
        own = pick(own, y, 1) + b.astype(F32) + a.astype(F32)
    return down_z(own, kind)


def weight_grad(left, grad, x_first):
    n, m = lax.axis_size("seq"), lax.axis_size("dp")
    wide = left.shape[1] // n
    if (n, m) != (4, 8):
        part = lax.psum_scatter(product_t(left, grad), "seq", scatter_dimension=0, tiled=True)
        return lax.psum_scatter(part, "dp", scatter_dimension=0, tiled=True)

    def block(i):
        return product_t(lax.dynamic_slice_in_dim(left, i * wide, wide, 1), grad)

    return scatter_sum(block, wide // m, BF, x_first)


def small_grad(whole):
    n, m = lax.axis_size("seq"), lax.axis_size("dp")
    if (n, m) != (4, 8):
        part = lax.psum_scatter(whole, "seq", scatter_dimension=0, tiled=True)
        return lax.psum_scatter(part, "dp", scatter_dimension=0, tiled=True)
    wide = whole.shape[0] // n

    def block(i):
        return lax.dynamic_slice_in_dim(whole, i * wide, wide, 0)

    return scatter_sum(block, wide // m, F32, True)


def renew(weight, moment, average, grad, factor, tokens):
    rate = factor / math.sqrt(tokens)
    moment = 0.9 * moment + grad
    weight = weight - rate * (grad + 0.9 * moment)
    average = 0.8 * average + 0.2 * weight
    return (weight, moment, average)


def local(block_input, out_grad, lengths, *state):
    params, moments, averages = state[0::3], state[1::3], state[2::3]
    vectors, mix_weights, ffn_key, ffn_recept, ffn_value, maa_down, maa_up, decay_down, decay_up = params
    length, width = block_input.shape[1:]
    tokens = length * lax.axis_size("seq") * lax.axis_size("dp")
    rank = maa_up.shape[1]
    n_vec, n_down, n_decay = vectors.shape[0], maa_down.shape[1], decay_down.shape[1]
    start = lengths[0, 0] - lax.axis_index("seq") * length
    follows = (jnp.arange(length) != start) & (
        (jnp.arange(length) > 0) | (lax.axis_index("seq") > 0)
    )
    follows = follows.astype(F32)[:, None]
    keep = (jnp.arange(length // CHUNK) * CHUNK != start).astype(F32)

    small = jnp.concatenate(
        [vectors.T, maa_down, maa_up.reshape(5 * rank, -1).T, decay_down, decay_up.T], axis=1
    )
    small = lax.all_gather(small, BOTH, axis=0, tiled=True)
    cuts = np.cumsum([n_vec, n_down, 5 * rank, n_decay, n_decay])
    vecs, down, up, ddown, dup = jnp.split(small, cuts[:-1], axis=1)
    vecs, up, dup = vecs.T, up.T, dup.T

    mix = lax.all_gather(mix_weights.astype(BF), BOTH, axis=1, tiled=True)
    fkey = lax.all_gather(ffn_key.astype(BF), BOTH, axis=0, tiled=True)
    fval = lax.all_gather(ffn_value.astype(BF), BOTH, axis=0, tiled=True)
    frec = lax.all_gather(ffn_recept.astype(BF), BOTH, axis=0, tiled=True)

    hidden = block_input[0].astype(F32)
    normed, pull_norm_one = jax.vjp(norm_first, hidden, vecs)
    incoming = send_rows(normed)
    (xkey, xval, xrec, xgate, logdec), pull_mix = jax.vjp(
        functools.partial(mix_inputs, follows=follows), normed, incoming, vecs, down, up, ddown, dup
    )
    xkey, xval, xrec, xgate = (v.astype(BF) for v in (xkey, xval, xrec, xgate))
    keys = product(xkey, mix[0])
    values = product(xval, mix[1])
    closing, carry = close(keep, keys, values, logdec)
    before = prefix(carry, closing, False)
    recept = product(xrec, mix[2])
    gate = product(xgate, mix[3])
    vec3 = vecs[9:12]
    raw, gated, score, states = forward(keep, recept, keys, values, logdec, gate, vec3, before)
    middle = hidden + product(gated, mix[4])

    second, pull_norm_two = jax.vjp(norm_second, middle, vecs)
    incoming_two = send_rows(second)
    (key_in, rec_in), pull_channel = jax.vjp(
        functools.partial(channel_inputs, follows=follows), second, incoming_two, vecs
    )
    key_in, rec_in = key_in.astype(BF), rec_in.astype(BF)
    positive = jnp.maximum(product(key_in, fkey), 0.0)
    squared = (positive * positive).astype(BF)
    kvals = product(squared, fval)
    sigma = jax.nn.sigmoid(product(rec_in, frec))
    block_output = middle + sigma * kvals

    upstream = out_grad[0].astype(F32)
    grad_kvals = (upstream * sigma).astype(BF)
    grad_rpre = (upstream * kvals * sigma * (1.0 - sigma)).astype(BF)
    sum_fval = weight_grad(squared, grad_kvals, True)
    grad_kpre = (back_product(grad_kvals, fval) * (2.0 * positive)).astype(BF)
    sum_fkey = weight_grad(key_in, grad_kpre, False)
    sum_frec = weight_grad(rec_in, grad_rpre, False)
    grad_second, grad_inc_two, vec_one = pull_channel(
        (back_product(grad_kpre, fkey), back_product(grad_rpre, frec))
    )
    grad_second = back_rows(grad_inc_two, grad_second)
    grad_mid, vec_two = pull_norm_two(grad_second)
    grad_middle = upstream + grad_mid
    grad_attn = grad_middle.astype(BF)
    sum_out = weight_grad(gated, grad_attn, True)
    grad_gated = back_product(grad_attn, mix[4])
    grad_raw, grad_gate, direct, vec_head = head_back(
        keep, recept, logdec, raw, gate, grad_gated, vec3
    )
    later = prefix(carry, direct, True)
    sum_gate = weight_grad(xgate, grad_gate, False)
    grad_xgate = back_product(grad_gate, mix[3])
    grad_rec, grad_key, grad_val, grad_dec, vec_bonus = backward(
        keep, recept, keys, values, logdec, grad_raw, score, states, later, vec3
    )
    sum_rec = weight_grad(xrec, grad_rec, True)
    sum_key = weight_grad(xkey, grad_key, False)
    sum_val = weight_grad(xval, grad_val, True)
    grad_normed, grad_inc, vec_mix, gdown, gup, gddown, gdup = pull_mix(
        (
            back_product(grad_key, mix[0]),
            back_product(grad_val, mix[1]),
            back_product(grad_rec, mix[2]),
            grad_xgate,
            grad_dec,
        )
    )
    grad_normed = back_rows(grad_inc, grad_normed)
    grad_hidden, vec_three = pull_norm_one(grad_normed)
    input_grad = grad_middle + grad_hidden

    vec_all = vec_one + vec_two + vec_mix + vec_three
    vec_all = jnp.concatenate(
        [vec_all[:9], vec_all[9:10] + vec_bonus, vec_all[10:12] + vec_head, vec_all[12:]], axis=0
    )
    total = small_grad(jnp.concatenate([vec_all.T, gdown, gup.T, gddown, gdup.T], axis=1))
    gvec, gdown, gup, gddown, gdup = jnp.split(total, cuts[:-1], axis=1)
    grads = (
        gvec.T,
        jnp.stack([sum_key, sum_val, sum_rec, sum_gate, sum_out]),
        sum_fkey,
        sum_frec,
        sum_fval,
        gdown,
        gup.T.reshape(maa_up.shape),
        gddown,
        gdup.T,
    )
    results = [block_output[None], input_grad[None]]
    for param, moment, average, grad, factor in zip(params, moments, averages, grads, FACTORS):
        results.extend(renew(param, moment, average, grad, factor, tokens))
    return tuple(results)


def solution(mesh):
    vec, mix = P(None, BOTH), P(None, BOTH, None)
    rows, up = P(BOTH, None), P(None, None, BOTH)
    specs = [vec, mix, rows, rows, rows, rows, up, rows, vec]
    state = tuple(spec for spec in specs for _ in range(3))
    tokens = P("dp", "seq", None)
    return jax.shard_map(
        local,
        mesh=mesh,
        in_specs=(tokens, tokens, P("dp", None)) + state,
        out_specs=(tokens, tokens) + state,
        check_vma=False,
    )
```

```python
import functools
import math

import jax
import jax.numpy as jnp
import numpy as np
from jax import lax
from jax.experimental import pallas as pl
from jax.experimental.pallas import tpu as pltpu
from jax.sharding import PartitionSpec as P

HEAD = 64
LANES = 128
CHUNK = 64
BF = jnp.bfloat16
F32 = jnp.float32
NN = (((1,), (0,)), ((), ()))
NT = (((1,), (1,)), ((), ()))
TN = (((0,), (0,)), ((), ()))


def levels_of(chunk):
    return [1 << e for e in reversed(range(chunk.bit_length() - 1))]


def tables(chunk):
    levels = levels_of(chunk)
    at = np.arange(chunk)
    sums = []
    for m in levels[:-1]:
        same = at[:, None] // (2 * m) == at[None, :] // (2 * m)
        right = (at & m) > 0
        up = same & right[:, None] & right[None, :] & (at[None, :] < at[:, None])
        down = same & ~right[:, None] & ~right[None, :] & (at[None, :] > at[:, None])
        sums.append(up | down)
    sums.append(at[None, :] < at[:, None])
    sums.append(at[None, :] > at[:, None])
    sums = np.concatenate(sums, 0).astype(np.float32)
    level = np.full((chunk, chunk), -1, np.int32)
    for index, m in enumerate(levels):
        same = at[:, None] // (2 * m) == at[None, :] // (2 * m)
        right = (at & m) > 0
        level = np.where(same & (right[:, None] != right[None, :]), index, level)
    level = np.concatenate([level, level], 1)
    ones = (np.arange(LANES)[:, None] // HEAD == np.arange(LANES)[None, :] // HEAD).astype(np.float32)
    return sums, level, ones


def split(value, parts):
    pieces = []
    for _ in range(parts):
        piece = value.astype(BF)
        pieces.append(piece)
        value = value - piece.astype(F32)
    return pieces


def dot3(left, right, dims):
    lh, ll = left
    rh, rl = right
    la, ra = dims[0][0][0], dims[0][1][0]
    return lax.dot_general(
        jnp.concatenate([lh, lh, ll], la),
        jnp.concatenate([rh, rl, rh], ra),
        dims,
        preferred_element_type=F32,
    )


def two(value):
    return split(value, 2)


def spread(pieces, heads):
    return [jnp.where(heads, jnp.concatenate([p, p], 0), jnp.zeros((), p.dtype)) for p in pieces]


def exponents(sums_ref, ld, lo, hi):
    parts = jnp.concatenate(split(ld, 3), 0)
    c = sums_ref[lo:hi, :]
    return lax.dot_general(
        jnp.concatenate([c, c, c], 1), parts, NN, preferred_element_type=F32
    )


def head_mask(rows):
    r = lax.broadcasted_iota(jnp.int32, (2 * rows, LANES), 0) >= rows
    c = lax.broadcasted_iota(jnp.int32, (2 * rows, LANES), 1) >= HEAD
    return r == c


def head_sum(value, ones_ref):
    a, b = two(value)
    return lax.dot_general(
        jnp.concatenate([a, b], 1),
        jnp.concatenate([ones_ref[...], ones_ref[...]], 0),
        NN,
        preferred_element_type=F32,
    )


def silu(x):
    return x / (1.0 + jnp.exp(-x))


def close_kernel(keep_ref, k_ref, v_ref, ld_ref, sums_ref, state_ref, carry_ref):
    tokens = k_ref.shape[0]
    heads = head_mask(HEAD)
    state = jnp.zeros((LANES, LANES), F32)
    carry = jnp.ones((1, LANES), F32)
    n = sums_ref.shape[0] // CHUNK
    for c in range(tokens // CHUNK):
        rows = pl.ds(c * CHUNK, CHUNK)
        keep = keep_ref[c]
        ld = ld_ref[rows, :]
        e = exponents(sums_ref, ld, (n - 1) * CHUNK, n * CHUNK)
        last = jnp.exp(e[0:1] + ld[0:1]) * keep
        carry = carry * last
        fresh = dot3(two(v_ref[rows, :]), two(k_ref[rows, :] * jnp.exp(e)), TN)
        state = state * last + jnp.where(heads, fresh, 0.0)
    state_ref[...] = state[:HEAD] + state[HEAD:]
    carry_ref[...] = carry


def level_part(index, m, q, k, x):
    right = (lax.broadcasted_iota(jnp.int32, (CHUNK, LANES), 0) & m) > 0
    z = jnp.where(right, q, k)
    if m > 1:
        z = z * x[index * CHUNK : (index + 1) * CHUNK]
    return right, z


def forward_kernel(
    keep_ref, q_ref, k_ref, v_ref, ld_ref, gate_ref, vec_ref, start_ref, sums_ref, level_ref, ones_ref,
    raw_ref, gated_ref, score_ref, state_ref,
):
    tokens = q_ref.shape[0]
    levels = levels_of(CHUNK)
    n = sums_ref.shape[0] // CHUNK
    heads = head_mask(HEAD)
    wide = head_mask(CHUNK)
    level = level_ref[...]
    t = lax.broadcasted_iota(jnp.int32, (CHUNK, 2 * CHUNK), 0)
    s = lax.broadcasted_iota(jnp.int32, (CHUNK, 2 * CHUNK), 1) & (CHUNK - 1)
    bonus = vec_ref[0:1]
    state = jnp.where(heads, jnp.concatenate([start_ref[...], start_ref[...]], 0), 0.0)
    for c in range(tokens // CHUNK):
        rows = pl.ds(c * CHUNK, CHUNK)
        state = state * keep_ref[c]
        state_ref[pl.ds(c * HEAD, HEAD), :] = state[:HEAD] + state[HEAD:]
        q, k, v, ld = q_ref[rows, :], k_ref[rows, :], v_ref[rows, :], ld_ref[rows, :]
        e = exponents(sums_ref, ld, 0, n * CHUNK)
        x = jnp.exp(e)
        score = jnp.zeros((CHUNK, 2 * CHUNK), F32)
        for index, m in enumerate(levels):
            right, z = level_part(index, m, q, k, x)
            z = two(z)
            score = jnp.where(level == index, dot3(z, spread(z, wide), NT), score)
        score = jnp.where(t > s, score, 0.0)
        score = jnp.where(t == s, head_sum(q * bonus * k, ones_ref), score)
        score_ref[rows, :] = score
        xq, xk = x[(n - 2) * CHUNK : (n - 1) * CHUNK], x[(n - 1) * CHUNK :]
        v2 = two(v)
        raw = dot3(two(score), spread(v2, wide), NN) + dot3(two(q * xq), two(state), NT)
        last = jnp.exp(e[(n - 1) * CHUNK : (n - 1) * CHUNK + 1] + ld[0:1])
        state = state * last + jnp.where(heads, dot3(v2, two(k * xk), TN), 0.0)
        raw_ref[rows, :] = raw
        center = raw - head_sum(raw, ones_ref) * (1.0 / HEAD)
        spread_of = head_sum(center * center, ones_ref) * (1.0 / HEAD)
        normal = center * lax.rsqrt(spread_of + 0.00064)
        gated_ref[rows, :] = ((normal * vec_ref[1:2] + vec_ref[2:3]) * silu(gate_ref[rows, :])).astype(BF)


def head_back_kernel(
    keep_ref, q_ref, ld_ref, raw_ref, gate_ref, grad_ref, vec_ref, sums_ref, ones_ref,
    draw_ref, dgate_ref, direct_ref, dvec_ref,
):
    tokens = q_ref.shape[0]
    n = sums_ref.shape[0] // CHUNK
    heads = head_mask(HEAD)
    direct = jnp.zeros((LANES, LANES), F32)
    gain, bias = vec_ref[1:2], vec_ref[2:3]
    dgain = jnp.zeros((1, LANES), F32)
    dbias = jnp.zeros((1, LANES), F32)
    for c in reversed(range(tokens // CHUNK)):
        rows = pl.ds(c * CHUNK, CHUNK)
        raw, gate, grad = raw_ref[rows, :], gate_ref[rows, :], grad_ref[rows, :]
        center = raw - head_sum(raw, ones_ref) * (1.0 / HEAD)
        inv = lax.rsqrt(head_sum(center * center, ones_ref) * (1.0 / HEAD) + 0.00064)
        normal = center * inv
        sig = 1.0 / (1.0 + jnp.exp(-gate))
        act = gate * sig
        affine = normal * gain + bias
        dgate_ref[rows, :] = (grad * affine * (sig + act * (1.0 - sig))).astype(BF)
        daff = grad * act
        dgain = dgain + jnp.sum(daff * normal, 0, keepdims=True)
        dbias = dbias + jnp.sum(daff, 0, keepdims=True)
        dnorm = daff * gain
        draw = inv * (
            dnorm
            - head_sum(dnorm, ones_ref) * (1.0 / HEAD)
            - normal * (head_sum(dnorm * normal, ones_ref) * (1.0 / HEAD))
        )
        draw_ref[rows, :] = draw
        ld = ld_ref[rows, :]
        e = exponents(sums_ref, ld, (n - 2) * CHUNK, (n - 1) * CHUNK)
        last = jnp.exp(e[CHUNK - 1 :] + ld[CHUNK - 1 :])
        fresh = dot3(two(draw), two(q_ref[rows, :] * jnp.exp(e)), TN)
        direct = (direct * last + jnp.where(heads, fresh, 0.0)) * keep_ref[c]
    direct_ref[...] = direct[:HEAD] + direct[HEAD:]
    dvec_ref[0:1] = dgain
    dvec_ref[1:2] = dbias


def backward_kernel(
    keep_ref, q_ref, k_ref, v_ref, ld_ref, draw_ref, score_ref, state_ref, later_ref, vec_ref,
    sums_ref, sums_t_ref, level_ref, ones_ref,
    dq_ref, dk_ref, dv_ref, dld_ref, du_ref,
):
    tokens = q_ref.shape[0]
    levels = levels_of(CHUNK)
    n = sums_ref.shape[0] // CHUNK
    heads = head_mask(HEAD)
    wide = head_mask(CHUNK)
    level = level_ref[...]
    t = lax.broadcasted_iota(jnp.int32, (CHUNK, 2 * CHUNK), 0)
    s = lax.broadcasted_iota(jnp.int32, (CHUNK, 2 * CHUNK), 1) & (CHUNK - 1)
    lower = t > s
    bonus = vec_ref[0:1]
    dstate = jnp.where(heads, jnp.concatenate([later_ref[...], later_ref[...]], 0), 0.0)
    du = jnp.zeros((1, LANES), F32)
    for c in reversed(range(tokens // CHUNK)):
        rows = pl.ds(c * CHUNK, CHUNK)
        small = state_ref[pl.ds(c * HEAD, HEAD), :]
        state = jnp.where(heads, jnp.concatenate([small, small], 0), 0.0)
        q, k, v, ld = q_ref[rows, :], k_ref[rows, :], v_ref[rows, :], ld_ref[rows, :]
        draw = draw_ref[rows, :]
        e = exponents(sums_ref, ld, 0, n * CHUNK)
        x = jnp.exp(e)
        v2, draw2 = two(v), two(draw)
        dscore = jnp.where(
            lower, dot3(draw2, spread(v2, wide), NT), dot3(v2, spread(draw2, wide), NT)
        )
        dbon = head_sum(draw * v, ones_ref) * bonus
        dq = dbon * k
        dk = dbon * q
        du = du + jnp.sum(head_sum(draw * v, ones_ref) * q * k, 0, keepdims=True)
        grads = []
        for index, m in enumerate(levels):
            right, z = level_part(index, m, q, k, x)
            dz = dot3(
                two(jnp.where(level == index, dscore, 0.0)), spread(two(z), wide), NN
            )
            if m > 1:
                grads.append(z * dz)
                dz = dz * x[index * CHUNK : (index + 1) * CHUNK]
            dq = dq + jnp.where(right, dz, 0.0)
            dk = dk + jnp.where(right, 0.0, dz)
        xq, xk = x[(n - 2) * CHUNK : (n - 1) * CHUNK], x[(n - 1) * CHUNK :]
        qx, kx = q * xq, k * xk
        dstate2 = two(dstate)
        dqx = dot3(draw2, two(state), NN)
        dkx = dot3(v2, dstate2, NN)
        grads.append(dqx * qx)
        grads.append(dkx * kx)
        dq_ref[rows, :] = (dq + dqx * xq).astype(dq_ref.dtype)
        dk_ref[rows, :] = (dk + dkx * xk).astype(dk_ref.dtype)
        back = dot3(two(score_ref[rows, :]), draw2, TN)
        back = jnp.where(wide, back, 0.0)
        dv_ref[rows, :] = (back[:CHUNK] + back[CHUNK:] + dot3(two(kx), dstate2, NT)).astype(dv_ref.dtype)
        last = jnp.exp(e[(n - 1) * CHUNK : (n - 1) * CHUNK + 1] + ld[0:1])
        through = jnp.sum(state * dstate, 0, keepdims=True) * last
        gh, gl = two(jnp.concatenate(grads, 0))
        ct = sums_t_ref[...]
        dld_ref[rows, :] = through + lax.dot_general(
            jnp.concatenate([ct, ct], 1), jnp.concatenate([gh, gl], 0), NN, preferred_element_type=F32
        )
        dstate = dstate * last + jnp.where(heads, dot3(draw2, two(qx), TN), 0.0)
        dstate = dstate * keep_ref[c]
    du_ref[...] = du


def _call(kernel, outs, ins, tokens, width, flops):
    def spec(kind):
        kind, rows = kind
        if kind == "s":
            return pl.BlockSpec(memory_space=pltpu.SMEM)
        if kind == "c":
            return pl.BlockSpec(rows, lambda i: (0, 0))
        return pl.BlockSpec((rows, LANES), lambda i: (0, i))

    return pl.pallas_call(
        kernel,
        grid=(width // LANES,),
        in_specs=[spec(kind) for kind, _ in ins],
        out_specs=[spec(("r", rows)) for rows, _ in outs],
        out_shape=[jax.ShapeDtypeStruct((rows, width), dt) for rows, dt in outs],
        compiler_params=pltpu.CompilerParams(vmem_limit_bytes=48 * 2**20),
        cost_estimate=pl.CostEstimate(flops=flops, bytes_accessed=10 * tokens * width * 4, transcendentals=8 * tokens * width),
    )(*[value for _, value in ins])


def rows_of(value):
    return (("r", value.shape[0]), value)


def const_of(value):
    return (("c", value.shape), value)


def close(keep, k, v, ld):
    tokens, width = k.shape
    sums, _, _ = tables(CHUNK)
    return _call(
        close_kernel, [(HEAD, F32), (1, F32)],
        [(("s", 0), keep), rows_of(k), rows_of(v), rows_of(ld), const_of(jnp.asarray(sums, BF))],
        tokens, width, tokens * width * 2000,
    )


def forward(keep, q, k, v, ld, gate, vec3, start):
    tokens, width = k.shape
    sums, level, ones = tables(CHUNK)
    return _call(
        forward_kernel,
        [(tokens, F32), (tokens, BF), (tokens, F32), (tokens // CHUNK * HEAD, F32)],
        [(("s", 0), keep), rows_of(q), rows_of(k), rows_of(v), rows_of(ld), rows_of(gate), rows_of(vec3), rows_of(start),
         const_of(jnp.asarray(sums, BF)), const_of(jnp.asarray(level)), const_of(jnp.asarray(ones, BF))],
        tokens, width, tokens * width * 20000,
    )


def head_back(keep, q, ld, raw, gate, grad, vec3):
    tokens, width = q.shape
    sums, level, ones = tables(CHUNK)
    return _call(
        head_back_kernel,
        [(tokens, F32), (tokens, BF), (HEAD, F32), (2, F32)],
        [(("s", 0), keep), rows_of(q), rows_of(ld), rows_of(raw), rows_of(gate), rows_of(grad), rows_of(vec3),
         const_of(jnp.asarray(sums, BF)), const_of(jnp.asarray(ones, BF))],
        tokens, width, tokens * width * 4000,
    )


def backward(keep, q, k, v, ld, draw, score, state, later, vec3):
    tokens, width = q.shape
    sums, level, ones = tables(CHUNK)
    return _call(
        backward_kernel,
        [(tokens, BF), (tokens, BF), (tokens, BF), (tokens, F32), (1, F32)],
        [(("s", 0), keep), rows_of(q), rows_of(k), rows_of(v), rows_of(ld), rows_of(draw), rows_of(score), rows_of(state),
         rows_of(later), rows_of(vec3), const_of(jnp.asarray(sums, BF)), const_of(jnp.asarray(sums.T.copy(), BF)),
         const_of(jnp.asarray(level)), const_of(jnp.asarray(ones, BF))],
        tokens, width, tokens * width * 30000,
    )


HIGHEST = lax.Precision.HIGHEST
FACTORS = (0.2, 0.03, 0.03, 0.03, 0.03, 0.03, 0.03, 0.03, 0.03)
BOTH = ("seq", "dp")


def layer_norm(field, gain, bias):
    center = field - jnp.mean(field, axis=-1, keepdims=True)
    spread_of = jnp.mean(center * center, axis=-1, keepdims=True)
    return center * lax.rsqrt(spread_of + 1e-05) * gain + bias


def norm_first(field, vecs):
    return layer_norm(field, vecs[0], vecs[1])


def norm_second(field, vecs):
    return layer_norm(field, vecs[12], vecs[13])


def shifted(field, incoming, follows):
    return jnp.concatenate([incoming, field[:-1]], axis=0) * follows


def mix_inputs(normed, incoming, vecs, down, up, ddown, dup, follows):
    delta = shifted(normed, incoming, follows) - normed
    lora = jnp.tanh(jnp.dot(normed + delta * vecs[2], down, precision=HIGHEST))
    rank = lora.shape[1] // 5
    inputs = [
        normed
        + delta
        * (
            vecs[3 + c]
            + jnp.dot(
                lora[:, c * rank : (c + 1) * rank], up[c * rank : (c + 1) * rank], precision=HIGHEST
            )
        )
        for c in range(5)
    ]
    decay = vecs[8] + jnp.dot(
        jnp.tanh(jnp.dot(inputs[0], ddown, precision=HIGHEST)), dup, precision=HIGHEST
    )
    return (inputs[1], inputs[2], inputs[3], inputs[4], -jnp.exp(decay))


def channel_inputs(second, incoming, vecs, follows):
    delta = shifted(second, incoming, follows) - second
    return (second + delta * vecs[14], second + delta * vecs[15])


def send_rows(field):
    n = lax.axis_size("seq")
    return lax.ppermute(field[-1:], "seq", [(i, i + 1) for i in range(n - 1)])


def back_rows(grad_first, field):
    n = lax.axis_size("seq")
    arrived = lax.ppermute(grad_first, "seq", [(i + 1, i) for i in range(n - 1)])
    last = lax.broadcasted_iota(jnp.int32, field.shape, 0) == field.shape[0] - 1
    return field + jnp.where(last, arrived, 0.0)


def prefix(carry, state, reverse):
    n, here = lax.axis_size("seq"), lax.axis_index("seq")
    own = jnp.concatenate([state, carry], 0)
    if not tuned():
        every = lax.all_gather(own, "seq")
        total = jnp.zeros_like(state)
        for k in range(n):
            at = n - 1 - k if reverse else k
            reached = at > here if reverse else at < here
            total = jnp.where(reached, every[at, -1:] * total + every[at, :-1], total)
        return total
    other = swap(own, "seq", 1)
    other_state, other_carry = other[:-1], other[-1:]
    second = (here % 2 == 1) != reverse
    chip = jnp.where(second, carry * other_state + state, other_carry * state + other_state)
    pairs = [(2, 0), (3, 1)] if reverse else [(0, 2), (1, 3)]
    arrived = lax.ppermute(chip, "seq", pairs)
    return jnp.where(second, other_carry * arrived + other_state, arrived)


def product(left, right):
    return jnp.dot(left, right, preferred_element_type=F32)


def product_t(left, right):
    return lax.dot_general(left, right, TN, preferred_element_type=F32)


def back_product(grad, weight):
    return lax.dot_general(grad, weight, NT, preferred_element_type=F32)


def swap(value, axis, bit):
    return lax.ppermute(value, axis, [(i, i ^ bit) for i in range(lax.axis_size(axis))])


def to_plane(value, step):
    n = lax.axis_size("dp")
    return lax.ppermute(value, "dp", [(i, (i + 2 * step) % n) for i in range(n)])


def pick(value, index, axis=0):
    return lax.dynamic_index_in_dim(value, index, axis, keepdims=False)


def tuned():
    return (lax.axis_size("seq"), lax.axis_size("dp")) == (4, 8)


class Steps:
    def __init__(self):
        self.units = []

    def add(self, *units):
        self.units.extend([unit, None, None] for unit in units)
        return self.units[-len(units) :]

    def tick(self, values=()):
        live = [u for u in self.units if u[0] is not None]
        waiting, values = lax.optimization_barrier(([u[1] for u in live], values))
        for unit, arrived in zip(live, waiting):
            try:
                unit[1] = unit[0].send(arrived)
            except StopIteration as stop:
                unit[:] = [None, None, stop.value]
        return values

    def drain(self):
        while any(u[0] is not None for u in self.units):
            self.tick()


def gather_unit(shard):
    d = lax.axis_index("dp")
    z, y = d // 2, d % 2
    arrived = yield [to_plane(shard, t) for t in (1, 2, 3)]
    column = jnp.stack([shard, *arrived])
    (other,) = yield [swap(column, "dp", 1)]
    both = jnp.concatenate([column, other], 0)
    chunks = [pick(both, ((k ^ y) * 4) + (z - j) % 4) for j in range(4) for k in (0, 1)]
    slab = jnp.concatenate(chunks, 0)
    across, near = yield [swap(slab, "seq", 2), swap(slab, "seq", 1)]
    (far,) = yield [swap(across, "seq", 1)]
    return [slab, near, across, far]


def plain_gather(shard):
    return [lax.all_gather(shard, BOTH, axis=0, tiled=True)]
    yield


def gather(shard):
    return gather_unit(shard) if tuned() else plain_gather(shard)


def in_order(pieces):
    if not tuned():
        return pieces[0]
    s, every = lax.axis_index("seq"), jnp.stack(pieces)
    return jnp.concatenate([pick(every, s ^ j) for j in range(4)])


def scatter_unit(first, second, rows, kind):
    s, d = lax.axis_index("seq"), lax.axis_index("dp")
    z, y = d // 2, d % 2
    wide = rows * 8

    def parts(value):
        return value.reshape(-1, 4, 2, rows, value.shape[-1])

    sends = [swap(f([s ^ 3, s ^ 1]).astype(kind), "seq", 1) for f in (first, second) if f]
    one, *two = yield sends
    sends = [swap((first([s ^ 2]) + one[:wide].astype(F32)).astype(kind), "seq", 2)]
    if second:
        both = parts((second([s ^ 2, s]) + two[0].astype(F32)).astype(kind))
        sends.append(swap(pick(both, 1 - y, 2), "dp", 1))
    across, *beside = yield sends
    own = parts((first([s]) + one[wide:].astype(F32) + across.astype(F32)).astype(kind))
    sends = [swap(pick(own, 1 - y, 2), "dp", 1)]
    if second:
        both = pick(both, y, 2).astype(F32) + beside[0].astype(F32)
        sends.append(swap(both[0].astype(kind), "seq", 2))
    beside, *across = yield sends
    own = [(pick(own, y, 2)[0].astype(F32) + beside[0].astype(F32)).astype(kind)]
    if second:
        own.append((both[1] + across[0].astype(F32)).astype(kind))
    own = jnp.stack(own, 1)
    arrived = yield [to_plane(pick(own, (z + t) % 4), t) for t in (1, 2, 3)]
    total = pick(own, z).astype(F32)
    for part in arrived:
        total = total + part.astype(F32)
    return [total[i] for i in range(total.shape[0])]


def plain_scatter(*wholes):
    results = []
    for whole in wholes:
        part = lax.psum_scatter(whole, "seq", scatter_dimension=0, tiled=True)
        results.append(lax.psum_scatter(part, "dp", scatter_dimension=0, tiled=True))
    return results
    yield


def scatter(*pairs):
    if not tuned():
        return plain_scatter(*[product_t(left, grad) for left, grad in pairs])

    def blocks(left, grad):
        wide = left.shape[1] // 4

        def block(shards):
            taken = [lax.dynamic_slice_in_dim(left, i * wide, wide, 1) for i in shards]
            return product_t(jnp.concatenate(taken, 1), grad)

        return block

    if len(pairs) == 1:
        left, grad = pairs[0]
        half = grad.shape[1] // 2
        pairs = ((left, grad[:, :half]), (left, grad[:, half:]))
    rows = pairs[0][0].shape[1] // 4 // lax.axis_size("dp")
    return scatter_unit(*[blocks(*pair) for pair in pairs], rows, BF)


def scatter_small(whole):
    if not tuned():
        return plain_scatter(whole)
    wide = whole.shape[0] // 4

    def block(shards):
        return jnp.concatenate([lax.dynamic_slice_in_dim(whole, i * wide, wide, 0) for i in shards])

    return scatter_unit(block, None, wide // 8, F32)


def renew(weight, moment, average, grad, factor, tokens):
    rate = factor / math.sqrt(tokens)
    moment = 0.9 * moment + grad
    weight = weight - rate * (grad + 0.9 * moment)
    average = 0.8 * average + 0.2 * weight
    return (weight, moment, average)


def local(block_input, out_grad, lengths, *state):
    params, moments, averages = state[0::3], state[1::3], state[2::3]
    vectors, mix_weights, ffn_key, ffn_recept, ffn_value, maa_down, maa_up, decay_down, decay_up = params
    length, width = block_input.shape[1:]
    tokens = length * lax.axis_size("seq") * lax.axis_size("dp")
    rank = maa_up.shape[1]
    n_vec, n_down, n_decay = vectors.shape[0], maa_down.shape[1], decay_down.shape[1]
    start = lengths[0, 0] - lax.axis_index("seq") * length
    follows = (jnp.arange(length) != start) & (
        (jnp.arange(length) > 0) | (lax.axis_index("seq") > 0)
    )
    follows = follows.astype(F32)[:, None]
    keep = (jnp.arange(length // CHUNK) * CHUNK != start).astype(F32)

    small = jnp.concatenate(
        [vectors.T, maa_down, maa_up.reshape(5 * rank, -1).T, decay_down, decay_up.T], axis=1
    )
    up_steps = Steps()
    (small,) = up_steps.add(gather(small))
    up_steps.drain()
    mix = lax.all_gather(mix_weights.astype(BF), BOTH, axis=1, tiled=True)
    fkey = lax.all_gather(ffn_key.astype(BF), BOTH, axis=0, tiled=True)
    fval = lax.all_gather(ffn_value.astype(BF), BOTH, axis=0, tiled=True)
    frec = lax.all_gather(ffn_recept.astype(BF), BOTH, axis=0, tiled=True)
    small = in_order(small[-1])
    cuts = np.cumsum([n_vec, n_down, 5 * rank, n_decay, n_decay])
    vecs, down, up, ddown, dup = jnp.split(small, cuts[:-1], axis=1)
    vecs, up, dup = vecs.T, up.T, dup.T

    hidden = block_input[0].astype(F32)
    normed, pull_norm_one = jax.vjp(norm_first, hidden, vecs)
    incoming = send_rows(normed)
    (xkey, xval, xrec, xgate, logdec), pull_mix = jax.vjp(
        functools.partial(mix_inputs, follows=follows), normed, incoming, vecs, down, up, ddown, dup
    )
    xkey, xval, xrec, xgate = (v.astype(BF) for v in (xkey, xval, xrec, xgate))
    keys = product(xkey, mix[0])
    values = product(xval, mix[1])
    closing, carry = close(keep, keys, values, logdec)
    before = prefix(carry, closing, False)
    recept = product(xrec, mix[2])
    gate = product(xgate, mix[3])
    vec3 = vecs[9:12]
    raw, gated, score, states = forward(keep, recept, keys, values, logdec, gate, vec3, before)
    middle = hidden + product(gated, mix[4])

    second, pull_norm_two = jax.vjp(norm_second, middle, vecs)
    incoming_two = send_rows(second)
    (key_in, rec_in), pull_channel = jax.vjp(
        functools.partial(channel_inputs, follows=follows), second, incoming_two, vecs
    )
    key_in, rec_in = key_in.astype(BF), rec_in.astype(BF)
    positive = jnp.maximum(product(key_in, fkey), 0.0)
    squared = (positive * positive).astype(BF)
    kvals = product(squared, fval)
    sigma = jax.nn.sigmoid(product(rec_in, frec))
    block_output = middle + sigma * kvals

    steps = Steps()
    upstream = out_grad[0].astype(F32)
    grad_kvals = (upstream * sigma).astype(BF)
    grad_rpre = (upstream * kvals * sigma * (1.0 - sigma)).astype(BF)
    (sum_fval,) = steps.add(scatter((squared, grad_kvals)))
    grad_kvals = steps.tick(grad_kvals)
    grad_kpre = (back_product(grad_kvals, fval) * (2.0 * positive)).astype(BF)
    grad_kpre = steps.tick(grad_kpre)
    grad_second, grad_inc_two, vec_one = pull_channel(
        (back_product(grad_kpre, fkey), back_product(grad_rpre, frec))
    )
    grad_second = back_rows(grad_inc_two, grad_second)
    grad_mid, vec_two = pull_norm_two(grad_second)
    grad_middle = upstream + grad_mid
    grad_attn = grad_middle.astype(BF)
    (sum_fkey,) = steps.add(scatter((key_in, grad_kpre)))
    grad_attn = steps.tick(grad_attn)
    grad_gated = back_product(grad_attn, mix[4])
    grad_raw, grad_gate, direct, vec_head = head_back(
        keep, recept, logdec, raw, gate, grad_gated, vec3
    )
    later = prefix(carry, direct, True)
    later, grad_gate = steps.tick((later, grad_gate))
    grad_xgate = back_product(grad_gate, mix[3])
    grad_rec, grad_key, grad_val, grad_dec, vec_bonus = backward(
        keep, recept, keys, values, logdec, grad_raw, score, states, later, vec3
    )
    (sum_rec_out,) = steps.add(scatter((rec_in, grad_rpre), (gated, grad_attn)))
    grad_rec, grad_key, grad_val, grad_xgate = steps.tick(
        (grad_rec, grad_key, grad_val, grad_xgate)
    )
    grad_x = (
        back_product(grad_key, mix[0]),
        back_product(grad_val, mix[1]),
        back_product(grad_rec, mix[2]),
        grad_xgate,
        grad_dec,
    )
    grad_x = steps.tick(grad_x)
    grad_normed, grad_inc, vec_mix, gdown, gup, gddown, gdup = pull_mix(grad_x)
    grad_normed = back_rows(grad_inc, grad_normed)
    grad_hidden, vec_three = pull_norm_one(grad_normed)
    input_grad = grad_middle + grad_hidden

    vec_all = vec_one + vec_two + vec_mix + vec_three
    vec_all = jnp.concatenate(
        [vec_all[:9], vec_all[9:10] + vec_bonus, vec_all[10:12] + vec_head, vec_all[12:]], axis=0
    )
    total = jnp.concatenate([vec_all.T, gdown, gup.T, gddown, gdup.T], axis=1)
    (sum_gate_rec,) = steps.add(scatter((xgate, grad_gate), (xrec, grad_rec)))
    total, input_grad = steps.tick((total, input_grad))
    (sum_small,) = steps.add(scatter_small(total))
    steps.tick()
    (sum_key_val,) = steps.add(scatter((xkey, grad_key), (xval, grad_val)))
    steps.drain()

    gvec, gdown, gup, gddown, gdup = jnp.split(sum_small[-1][0], cuts[:-1], axis=1)
    grad_frec, grad_out = sum_rec_out[-1]
    grads = (
        gvec.T,
        jnp.stack([*sum_key_val[-1], sum_gate_rec[-1][1], sum_gate_rec[-1][0], grad_out]),
        jnp.concatenate(sum_fkey[-1], 1),
        grad_frec,
        jnp.concatenate(sum_fval[-1], 1),
        gdown,
        gup.T.reshape(maa_up.shape),
        gddown,
        gdup.T,
    )
    results = [block_output[None], input_grad[None]]
    for param, moment, average, grad, factor in zip(params, moments, averages, grads, FACTORS):
        results.extend(renew(param, moment, average, grad, factor, tokens))
    return tuple(results)


def solution(mesh):
    vec, mix = P(None, BOTH), P(None, BOTH, None)
    rows, up = P(BOTH, None), P(None, None, BOTH)
    specs = [vec, mix, rows, rows, rows, rows, up, rows, vec]
    state = tuple(spec for spec in specs for _ in range(3))
    tokens = P("dp", "seq", None)
    return jax.shard_map(
        local,
        mesh=mesh,
        in_specs=(tokens, tokens, P("dp", None)) + state,
        out_specs=(tokens, tokens) + state,
        check_vma=False,
    )
```

```python
import functools
import math

import jax
import jax.numpy as jnp
import numpy as np
from jax import lax
from jax.experimental import pallas as pl
from jax.experimental.pallas import tpu as pltpu
from jax.sharding import PartitionSpec as P

HEAD = 64
LANES = 128
CHUNK = 64
BF = jnp.bfloat16
F32 = jnp.float32
NN = (((1,), (0,)), ((), ()))
NT = (((1,), (1,)), ((), ()))
TN = (((0,), (0,)), ((), ()))


def levels_of(chunk):
    return [1 << e for e in reversed(range(chunk.bit_length() - 1))]


def tables(chunk):
    levels = levels_of(chunk)
    at = np.arange(chunk)
    sums = []
    for m in levels[:-1]:
        same = at[:, None] // (2 * m) == at[None, :] // (2 * m)
        right = (at & m) > 0
        up = same & right[:, None] & right[None, :] & (at[None, :] < at[:, None])
        down = same & ~right[:, None] & ~right[None, :] & (at[None, :] > at[:, None])
        sums.append(up | down)
    sums.append(at[None, :] < at[:, None])
    sums.append(at[None, :] > at[:, None])
    sums = np.concatenate(sums, 0).astype(np.float32)
    level = np.full((chunk, chunk), -1, np.int32)
    for index, m in enumerate(levels):
        same = at[:, None] // (2 * m) == at[None, :] // (2 * m)
        right = (at & m) > 0
        level = np.where(same & (right[:, None] != right[None, :]), index, level)
    level = np.concatenate([level, level], 1)
    ones = (np.arange(LANES)[:, None] // HEAD == np.arange(LANES)[None, :] // HEAD).astype(np.float32)
    return sums, level, ones


def split(value, parts):
    pieces = []
    for _ in range(parts):
        piece = value.astype(BF)
        pieces.append(piece)
        value = value - piece.astype(F32)
    return pieces


def dot3(left, right, dims):
    lh, ll = left
    rh, rl = right
    la, ra = dims[0][0][0], dims[0][1][0]
    return lax.dot_general(
        jnp.concatenate([lh, lh, ll], la),
        jnp.concatenate([rh, rl, rh], ra),
        dims,
        preferred_element_type=F32,
    )


def two(value):
    return split(value, 2)


def spread(pieces, heads):
    return [jnp.where(heads, jnp.concatenate([p, p], 0), jnp.zeros((), p.dtype)) for p in pieces]


def exponents(sums_ref, ld, lo, hi):
    parts = jnp.concatenate(split(ld, 3), 0)
    c = sums_ref[lo:hi, :]
    return lax.dot_general(
        jnp.concatenate([c, c, c], 1), parts, NN, preferred_element_type=F32
    )


def head_mask(rows):
    r = lax.broadcasted_iota(jnp.int32, (2 * rows, LANES), 0) >= rows
    c = lax.broadcasted_iota(jnp.int32, (2 * rows, LANES), 1) >= HEAD
    return r == c


def head_sum(value, ones_ref):
    a, b = two(value)
    return lax.dot_general(
        jnp.concatenate([a, b], 1),
        jnp.concatenate([ones_ref[...], ones_ref[...]], 0),
        NN,
        preferred_element_type=F32,
    )


def silu(x):
    return x / (1.0 + jnp.exp(-x))


def close_kernel(keep_ref, k_ref, v_ref, ld_ref, sums_ref, state_ref, carry_ref):
    tokens = k_ref.shape[0]
    heads = head_mask(HEAD)
    state = jnp.zeros((LANES, LANES), F32)
    carry = jnp.ones((1, LANES), F32)
    n = sums_ref.shape[0] // CHUNK
    for c in range(tokens // CHUNK):
        rows = pl.ds(c * CHUNK, CHUNK)
        keep = keep_ref[c]
        ld = ld_ref[rows, :]
        e = exponents(sums_ref, ld, (n - 1) * CHUNK, n * CHUNK)
        last = jnp.exp(e[0:1] + ld[0:1]) * keep
        carry = carry * last
        fresh = dot3(two(v_ref[rows, :]), two(k_ref[rows, :] * jnp.exp(e)), TN)
        state = state * last + jnp.where(heads, fresh, 0.0)
    state_ref[...] = state[:HEAD] + state[HEAD:]
    carry_ref[...] = carry


def level_part(index, m, q, k, x):
    right = (lax.broadcasted_iota(jnp.int32, (CHUNK, LANES), 0) & m) > 0
    z = jnp.where(right, q, k)
    if m > 1:
        z = z * x[index * CHUNK : (index + 1) * CHUNK]
    return right, z


def forward_kernel(
    keep_ref, q_ref, k_ref, v_ref, ld_ref, gate_ref, vec_ref, start_ref, sums_ref, level_ref, ones_ref,
    raw_ref, gated_ref, score_ref, state_ref,
):
    tokens = q_ref.shape[0]
    levels = levels_of(CHUNK)
    n = sums_ref.shape[0] // CHUNK
    heads = head_mask(HEAD)
    wide = head_mask(CHUNK)
    level = level_ref[...]
    t = lax.broadcasted_iota(jnp.int32, (CHUNK, 2 * CHUNK), 0)
    s = lax.broadcasted_iota(jnp.int32, (CHUNK, 2 * CHUNK), 1) & (CHUNK - 1)
    bonus = vec_ref[0:1]
    state = jnp.where(heads, jnp.concatenate([start_ref[...], start_ref[...]], 0), 0.0)
    for c in range(tokens // CHUNK):
        rows = pl.ds(c * CHUNK, CHUNK)
        state = state * keep_ref[c]
        state_ref[pl.ds(c * HEAD, HEAD), :] = state[:HEAD] + state[HEAD:]
        q, k, v, ld = q_ref[rows, :], k_ref[rows, :], v_ref[rows, :], ld_ref[rows, :]
        e = exponents(sums_ref, ld, 0, n * CHUNK)
        x = jnp.exp(e)
        score = jnp.zeros((CHUNK, 2 * CHUNK), F32)
        for index, m in enumerate(levels):
            right, z = level_part(index, m, q, k, x)
            z = two(z)
            score = jnp.where(level == index, dot3(z, spread(z, wide), NT), score)
        score = jnp.where(t > s, score, 0.0)
        score = jnp.where(t == s, head_sum(q * bonus * k, ones_ref), score)
        score_ref[rows, :] = score
        xq, xk = x[(n - 2) * CHUNK : (n - 1) * CHUNK], x[(n - 1) * CHUNK :]
        v2 = two(v)
        raw = dot3(two(score), spread(v2, wide), NN) + dot3(two(q * xq), two(state), NT)
        last = jnp.exp(e[(n - 1) * CHUNK : (n - 1) * CHUNK + 1] + ld[0:1])
        state = state * last + jnp.where(heads, dot3(v2, two(k * xk), TN), 0.0)
        raw_ref[rows, :] = raw
        center = raw - head_sum(raw, ones_ref) * (1.0 / HEAD)
        spread_of = head_sum(center * center, ones_ref) * (1.0 / HEAD)
        normal = center * lax.rsqrt(spread_of + 0.00064)
        gated_ref[rows, :] = ((normal * vec_ref[1:2] + vec_ref[2:3]) * silu(gate_ref[rows, :])).astype(BF)


def head_back_kernel(
    keep_ref, q_ref, ld_ref, raw_ref, gate_ref, grad_ref, vec_ref, sums_ref, ones_ref,
    draw_ref, dgate_ref, direct_ref, dvec_ref,
):
    tokens = q_ref.shape[0]
    n = sums_ref.shape[0] // CHUNK
    heads = head_mask(HEAD)
    direct = jnp.zeros((LANES, LANES), F32)
    gain, bias = vec_ref[1:2], vec_ref[2:3]
    dgain = jnp.zeros((1, LANES), F32)
    dbias = jnp.zeros((1, LANES), F32)
    for c in reversed(range(tokens // CHUNK)):
        rows = pl.ds(c * CHUNK, CHUNK)
        raw, gate, grad = raw_ref[rows, :], gate_ref[rows, :], grad_ref[rows, :]
        center = raw - head_sum(raw, ones_ref) * (1.0 / HEAD)
        inv = lax.rsqrt(head_sum(center * center, ones_ref) * (1.0 / HEAD) + 0.00064)
        normal = center * inv
        sig = 1.0 / (1.0 + jnp.exp(-gate))
        act = gate * sig
        affine = normal * gain + bias
        dgate_ref[rows, :] = (grad * affine * (sig + act * (1.0 - sig))).astype(BF)
        daff = grad * act
        dgain = dgain + jnp.sum(daff * normal, 0, keepdims=True)
        dbias = dbias + jnp.sum(daff, 0, keepdims=True)
        dnorm = daff * gain
        draw = inv * (
            dnorm
            - head_sum(dnorm, ones_ref) * (1.0 / HEAD)
            - normal * (head_sum(dnorm * normal, ones_ref) * (1.0 / HEAD))
        )
        draw_ref[rows, :] = draw
        ld = ld_ref[rows, :]
        e = exponents(sums_ref, ld, (n - 2) * CHUNK, (n - 1) * CHUNK)
        last = jnp.exp(e[CHUNK - 1 :] + ld[CHUNK - 1 :])
        fresh = dot3(two(draw), two(q_ref[rows, :] * jnp.exp(e)), TN)
        direct = (direct * last + jnp.where(heads, fresh, 0.0)) * keep_ref[c]
    direct_ref[...] = direct[:HEAD] + direct[HEAD:]
    dvec_ref[0:1] = dgain
    dvec_ref[1:2] = dbias


def backward_kernel(
    keep_ref, q_ref, k_ref, v_ref, ld_ref, draw_ref, score_ref, state_ref, later_ref, vec_ref,
    sums_ref, sums_t_ref, level_ref, ones_ref,
    dq_ref, dk_ref, dv_ref, dld_ref, du_ref,
):
    tokens = q_ref.shape[0]
    levels = levels_of(CHUNK)
    n = sums_ref.shape[0] // CHUNK
    heads = head_mask(HEAD)
    wide = head_mask(CHUNK)
    level = level_ref[...]
    t = lax.broadcasted_iota(jnp.int32, (CHUNK, 2 * CHUNK), 0)
    s = lax.broadcasted_iota(jnp.int32, (CHUNK, 2 * CHUNK), 1) & (CHUNK - 1)
    lower = t > s
    bonus = vec_ref[0:1]
    dstate = jnp.where(heads, jnp.concatenate([later_ref[...], later_ref[...]], 0), 0.0)
    du = jnp.zeros((1, LANES), F32)
    for c in reversed(range(tokens // CHUNK)):
        rows = pl.ds(c * CHUNK, CHUNK)
        small = state_ref[pl.ds(c * HEAD, HEAD), :]
        state = jnp.where(heads, jnp.concatenate([small, small], 0), 0.0)
        q, k, v, ld = q_ref[rows, :], k_ref[rows, :], v_ref[rows, :], ld_ref[rows, :]
        draw = draw_ref[rows, :]
        e = exponents(sums_ref, ld, 0, n * CHUNK)
        x = jnp.exp(e)
        v2, draw2 = two(v), two(draw)
        dscore = jnp.where(
            lower, dot3(draw2, spread(v2, wide), NT), dot3(v2, spread(draw2, wide), NT)
        )
        dbon = head_sum(draw * v, ones_ref) * bonus
        dq = dbon * k
        dk = dbon * q
        du = du + jnp.sum(head_sum(draw * v, ones_ref) * q * k, 0, keepdims=True)
        grads = []
        for index, m in enumerate(levels):
            right, z = level_part(index, m, q, k, x)
            dz = dot3(
                two(jnp.where(level == index, dscore, 0.0)), spread(two(z), wide), NN
            )
            if m > 1:
                grads.append(z * dz)
                dz = dz * x[index * CHUNK : (index + 1) * CHUNK]
            dq = dq + jnp.where(right, dz, 0.0)
            dk = dk + jnp.where(right, 0.0, dz)
        xq, xk = x[(n - 2) * CHUNK : (n - 1) * CHUNK], x[(n - 1) * CHUNK :]
        qx, kx = q * xq, k * xk
        dstate2 = two(dstate)
        dqx = dot3(draw2, two(state), NN)
        dkx = dot3(v2, dstate2, NN)
        grads.append(dqx * qx)
        grads.append(dkx * kx)
        dq_ref[rows, :] = (dq + dqx * xq).astype(dq_ref.dtype)
        dk_ref[rows, :] = (dk + dkx * xk).astype(dk_ref.dtype)
        back = dot3(two(score_ref[rows, :]), draw2, TN)
        back = jnp.where(wide, back, 0.0)
        dv_ref[rows, :] = (back[:CHUNK] + back[CHUNK:] + dot3(two(kx), dstate2, NT)).astype(dv_ref.dtype)
        last = jnp.exp(e[(n - 1) * CHUNK : (n - 1) * CHUNK + 1] + ld[0:1])
        through = jnp.sum(state * dstate, 0, keepdims=True) * last
        gh, gl = two(jnp.concatenate(grads, 0))
        ct = sums_t_ref[...]
        dld_ref[rows, :] = through + lax.dot_general(
            jnp.concatenate([ct, ct], 1), jnp.concatenate([gh, gl], 0), NN, preferred_element_type=F32
        )
        dstate = dstate * last + jnp.where(heads, dot3(draw2, two(qx), TN), 0.0)
        dstate = dstate * keep_ref[c]
    du_ref[...] = du


def _call(kernel, outs, ins, tokens, width, flops):
    def spec(kind):
        kind, rows = kind
        if kind == "s":
            return pl.BlockSpec(memory_space=pltpu.SMEM)
        if kind == "c":
            return pl.BlockSpec(rows, lambda i: (0, 0))
        return pl.BlockSpec((rows, LANES), lambda i: (0, i))

    return pl.pallas_call(
        kernel,
        grid=(width // LANES,),
        in_specs=[spec(kind) for kind, _ in ins],
        out_specs=[spec(("r", rows)) for rows, _ in outs],
        out_shape=[jax.ShapeDtypeStruct((rows, width), dt) for rows, dt in outs],
        compiler_params=pltpu.CompilerParams(vmem_limit_bytes=48 * 2**20),
        cost_estimate=pl.CostEstimate(flops=0, bytes_accessed=0, transcendentals=0),
    )(*[value for _, value in ins])


def rows_of(value):
    return (("r", value.shape[0]), value)


def const_of(value):
    return (("c", value.shape), value)


def close(keep, k, v, ld):
    tokens, width = k.shape
    sums, _, _ = tables(CHUNK)
    return _call(
        close_kernel, [(HEAD, F32), (1, F32)],
        [(("s", 0), keep), rows_of(k), rows_of(v), rows_of(ld), const_of(jnp.asarray(sums, BF))],
        tokens, width, tokens * width * 2000,
    )


def forward(keep, q, k, v, ld, gate, vec3, start):
    tokens, width = k.shape
    sums, level, ones = tables(CHUNK)
    return _call(
        forward_kernel,
        [(tokens, F32), (tokens, BF), (tokens, F32), (tokens // CHUNK * HEAD, F32)],
        [(("s", 0), keep), rows_of(q), rows_of(k), rows_of(v), rows_of(ld), rows_of(gate), rows_of(vec3), rows_of(start),
         const_of(jnp.asarray(sums, BF)), const_of(jnp.asarray(level)), const_of(jnp.asarray(ones, BF))],
        tokens, width, tokens * width * 20000,
    )


def head_back(keep, q, ld, raw, gate, grad, vec3):
    tokens, width = q.shape
    sums, level, ones = tables(CHUNK)
    return _call(
        head_back_kernel,
        [(tokens, F32), (tokens, BF), (HEAD, F32), (2, F32)],
        [(("s", 0), keep), rows_of(q), rows_of(ld), rows_of(raw), rows_of(gate), rows_of(grad), rows_of(vec3),
         const_of(jnp.asarray(sums, BF)), const_of(jnp.asarray(ones, BF))],
        tokens, width, tokens * width * 4000,
    )


def backward(keep, q, k, v, ld, draw, score, state, later, vec3):
    tokens, width = q.shape
    sums, level, ones = tables(CHUNK)
    return _call(
        backward_kernel,
        [(tokens, BF), (tokens, BF), (tokens, BF), (tokens, F32), (1, F32)],
        [(("s", 0), keep), rows_of(q), rows_of(k), rows_of(v), rows_of(ld), rows_of(draw), rows_of(score), rows_of(state),
         rows_of(later), rows_of(vec3), const_of(jnp.asarray(sums, BF)), const_of(jnp.asarray(sums.T.copy(), BF)),
         const_of(jnp.asarray(level)), const_of(jnp.asarray(ones, BF))],
        tokens, width, tokens * width * 30000,
    )


def dot3s(left, right, dims):
    lh, ll = left
    rh, rl = right

    def one(a, b):
        return lax.dot_general(a, b, dims, preferred_element_type=F32)

    return one(lh, rh) + one(lh, rl) + one(ll, rh)


def mix_back_kernel(
    g1_ref, g2_ref, g3_ref, g4_ref, gld_ref, ld_ref, n_ref, p_ref, f_ref, vec_ref, lora_ref, tan_ref,
    down_ref, up_ref, ddown_ref, dup_ref,
    gn_ref, ginc_ref, gvec_ref, gdown_ref, gup_ref, gddown_ref, gdup_ref,
    gdl_ref, flat_ref,
):
    tokens, width = n_ref.shape
    rank, block = lora_ref.shape[2], 256
    tan = tan_ref[...]
    tan2 = two(tan)
    lora2 = [two(lora_ref[c]) for c in range(5)]

    def columns(j):
        return pl.ds(pl.multiple_of(j * block, block), block)

    def total(value):
        return jnp.sum(value, 0, keepdims=True)

    def first(j, carry):
        gtan, glora = carry
        at = columns(j)
        n = n_ref[:, at]
        d = p_ref[:, at] - n
        gdec = gld_ref[:, at] * ld_ref[:, at]
        gvec_ref[6:7, at] = total(gdec)
        gdec2 = two(gdec)
        gtan = gtan + dot3(gdec2, two(dup_ref[:, at]), NT)
        gdup_ref[:, at] = dot3(tan2, gdec2, TN)
        gn = jnp.zeros_like(n)
        gdl = jnp.zeros_like(n)
        new = []
        for c, ref in enumerate((g1_ref, g2_ref, g3_ref, g4_ref), 1):
            g = ref[:, at]
            up2 = two(up_ref[c, :, at])
            m = vec_ref[3 + c : 4 + c, at] + dot3s(lora2[c], up2, NN)
            gm = g * d
            gm2 = two(gm)
            gvec_ref[1 + c : 2 + c, at] = total(gm)
            gup_ref[c, :, at] = dot3(lora2[c], gm2, TN)
            new.append(glora[c - 1] + dot3(gm2, up2, NT))
            gn = gn + g
            gdl = gdl + g * m
        gn_ref[:, at] = gn
        gdl_ref[:, at] = gdl
        return gtan, tuple(new)

    blank = jnp.zeros((tokens, rank), F32)
    gtan, glora = lax.fori_loop(0, width // block, first, (jnp.zeros_like(tan), (blank,) * 4))
    gtan2 = two(gtan * (1.0 - tan * tan))

    def second(j, glora):
        at = columns(j)
        n = n_ref[:, at]
        d = p_ref[:, at] - n
        g = dot3s(gtan2, two(ddown_ref[at, :]), NT)
        up2 = two(up_ref[0, :, at])
        m = vec_ref[3:4, at] + dot3s(lora2[0], up2, NN)
        gddown_ref[at, :] = dot3(two(n + d * m), gtan2, TN)
        gm = g * d
        gm2 = two(gm)
        gvec_ref[1:2, at] = total(gm)
        gup_ref[0, :, at] = dot3(lora2[0], gm2, TN)
        gn_ref[:, at] += g
        gdl_ref[:, at] += g * m
        return glora + dot3(gm2, up2, NT)

    glora = (lax.fori_loop(0, width // block, second, blank), *glora)
    for c in range(5):
        lora = lora_ref[c]
        flat_ref[:, c * rank : (c + 1) * rank] = glora[c] * (1.0 - lora * lora)
    flat2 = two(flat_ref[...])
    last = lax.broadcasted_iota(jnp.int32, (tokens, block), 0) == tokens - 1

    def third(j, carry):
        at = columns(j)
        n = n_ref[:, at]
        d = p_ref[:, at] - n
        shift = vec_ref[2:3, at]
        g = dot3s(flat2, two(down_ref[at, :]), NT)
        gdown_ref[at, :] = dot3(two(n + d * shift), flat2, TN)
        gvec_ref[0:1, at] = total(g * d)
        gdl = gdl_ref[:, at] + g * shift
        passed = gdl * f_ref[...]
        ginc_ref[:, at] = passed[0:1]
        passed = jnp.where(last, 0.0, pltpu.roll(passed, tokens - 1, 0))
        gn_ref[:, at] = gn_ref[:, at] + g - gdl + passed
        return carry

    lax.fori_loop(0, width // block, third, 0)
    gvec_ref[7:8, :] = jnp.zeros((1, width), F32)


def mix_back(grads, grad_dec, logdec, normed, prior, follows, vecs, lora, tan, down, up, ddown, dup):
    tokens, width = normed.shape
    rank = up.shape[1]
    lora = jnp.stack([lora[:, c * rank : (c + 1) * rank] for c in range(5)])
    shapes = [
        (tokens, width), (1, width), (8, width), down.shape, up.shape, ddown.shape, dup.shape,
    ]
    return pl.pallas_call(
        mix_back_kernel,
        in_specs=[pl.BlockSpec(memory_space=pltpu.VMEM)] * 16,
        out_specs=[pl.BlockSpec(memory_space=pltpu.VMEM)] * 7,
        out_shape=[jax.ShapeDtypeStruct(shape, F32) for shape in shapes],
        scratch_shapes=[pltpu.VMEM((tokens, width), F32), pltpu.VMEM((tokens, 5 * rank), F32)],
        compiler_params=pltpu.CompilerParams(vmem_limit_bytes=56 * 2**20),
        cost_estimate=pl.CostEstimate(flops=0, bytes_accessed=0, transcendentals=0),
    )(*grads, grad_dec, logdec, normed, prior, follows, vecs, lora, tan, down, up, ddown, dup)


FREE = pl.CostEstimate(flops=0, bytes_accessed=0, transcendentals=0)


def tile_of(size, largest):
    return max(t for t in range(128, largest + 1, 128) if size % t == 0)


def slab_kernel(index_ref, left_ref, grad_ref, *refs):
    total = lax.dot_general(left_ref[...], grad_ref[...], TN, preferred_element_type=F32)
    for ref in refs[:-1]:
        total = total + ref[...].astype(F32)
    refs[-1][...] = total.astype(refs[-1].dtype)


def slab_grad(left, grad, wide, start, width, shards, added=()):
    tokens = left.shape[0]
    tr, tc = tile_of(wide, 1024), tile_of(width, 2048)
    steps = wide // tr
    grid = (len(shards), steps, width // tc)
    return pl.pallas_call(
        slab_kernel,
        grid_spec=pltpu.PrefetchScalarGridSpec(
            num_scalar_prefetch=1,
            grid=grid,
            in_specs=[
                pl.BlockSpec((tokens, tr), lambda i, a, b, index: (0, index[i] * steps + a)),
                pl.BlockSpec((tokens, tc), lambda i, a, b, index: (0, start // tc + b)),
            ]
            + [
                pl.BlockSpec((tr, tc), functools.partial(_row_block, row // tr, steps))
                for _, row in added
            ],
            out_specs=pl.BlockSpec((tr, tc), functools.partial(_row_block, 0, steps)),
        ),
        out_shape=jax.ShapeDtypeStruct((len(shards) * wide, width), BF),
        compiler_params=pltpu.CompilerParams(vmem_limit_bytes=56 * 2**20),
        cost_estimate=FREE,
    )(jnp.stack(shards).astype(jnp.int32), left, grad, *[value for value, _ in added])


def _row_block(first, steps, i, a, b, index):
    return (first + i * steps + a, b)


def back_kernel(grad_ref, weight_ref, *refs):
    total = lax.dot_general(grad_ref[...], weight_ref[...], NT, preferred_element_type=F32)
    if len(refs) == 2:
        total = total * (2.0 * refs[0][...])
    refs[-1][...] = total.astype(refs[-1].dtype)


def back_dot(grad, weight, place=None, positive=None):
    tokens, width = grad.shape
    rows = weight.shape[-2]
    tile = tile_of(rows, 512 if width <= 4096 else 256)
    if place is None:
        spec = pl.BlockSpec((tile, width), lambda a: (a, 0))
    else:
        spec = pl.BlockSpec((None, tile, width), lambda a: (place, a, 0))
    column = pl.BlockSpec((tokens, tile), lambda a: (0, a))
    return pl.pallas_call(
        back_kernel,
        grid=(rows // tile,),
        in_specs=[pl.BlockSpec((tokens, width), lambda a: (0, 0)), spec]
        + [column] * (positive is not None),
        out_specs=column,
        out_shape=jax.ShapeDtypeStruct((tokens, rows), F32 if positive is None else BF),
        compiler_params=pltpu.CompilerParams(vmem_limit_bytes=56 * 2**20),
        cost_estimate=FREE,
    )(grad, weight, *([] if positive is None else [positive]))


HIGHEST = lax.Precision.HIGHEST
FACTORS = (0.2, 0.03, 0.03, 0.03, 0.03, 0.03, 0.03, 0.03, 0.03)
BOTH = ("seq", "dp")


def layer_norm(field, gain, bias):
    center = field - jnp.mean(field, axis=-1, keepdims=True)
    spread_of = jnp.mean(center * center, axis=-1, keepdims=True)
    return center * lax.rsqrt(spread_of + 1e-05) * gain + bias


def norm_first(field, vecs):
    return layer_norm(field, vecs[0], vecs[1])


def norm_second(field, vecs):
    return layer_norm(field, vecs[12], vecs[13])


def shifted(field, incoming, follows):
    return jnp.concatenate([incoming, field[:-1]], axis=0) * follows


def mix_inputs(normed, prior, vecs, down, up, ddown, dup):
    delta = prior - normed
    lora = jnp.tanh(jnp.dot(normed + delta * vecs[2], down, precision=HIGHEST))
    rank = up.shape[1]
    inputs = [
        normed
        + delta
        * (
            vecs[3 + c]
            + jnp.dot(lora[:, c * rank : (c + 1) * rank], up[c], precision=HIGHEST)
        )
        for c in range(5)
    ]
    tan = jnp.tanh(jnp.dot(inputs[0], ddown, precision=HIGHEST))
    logdec = -jnp.exp(vecs[8] + jnp.dot(tan, dup, precision=HIGHEST))
    return [v.astype(BF) for v in inputs[1:]], logdec, lora, tan


def channel_inputs(second, incoming, vecs, follows):
    delta = shifted(second, incoming, follows) - second
    return (second + delta * vecs[14], second + delta * vecs[15])


def send_rows(field):
    n = lax.axis_size("seq")
    return lax.ppermute(field[-1:], "seq", [(i, i + 1) for i in range(n - 1)])


def back_rows(grad_first, field):
    n = lax.axis_size("seq")
    arrived = lax.ppermute(grad_first, "seq", [(i + 1, i) for i in range(n - 1)])
    last = lax.broadcasted_iota(jnp.int32, field.shape, 0) == field.shape[0] - 1
    return field + jnp.where(last, arrived, 0.0)


def prefix(carry, state, reverse):
    n, here = lax.axis_size("seq"), lax.axis_index("seq")
    own = jnp.concatenate([state, carry], 0)
    if not tuned():
        every = lax.all_gather(own, "seq")
        total = jnp.zeros_like(state)
        for k in range(n):
            at = n - 1 - k if reverse else k
            reached = at > here if reverse else at < here
            total = jnp.where(reached, every[at, -1:] * total + every[at, :-1], total)
        return total
    other = swap(own, "seq", 1)
    other_state, other_carry = other[:-1], other[-1:]
    second = (here % 2 == 1) != reverse
    chip = jnp.where(second, carry * other_state + state, other_carry * state + other_state)
    pairs = [(2, 0), (3, 1)] if reverse else [(0, 2), (1, 3)]
    arrived = lax.ppermute(chip, "seq", pairs)
    return jnp.where(second, other_carry * arrived + other_state, arrived)


def product(left, right):
    return jnp.dot(left, right, preferred_element_type=F32)


def product_t(left, right):
    return lax.dot_general(left, right, TN, preferred_element_type=F32)


def back_product(grad, weight):
    return lax.dot_general(grad, weight, NT, preferred_element_type=F32)


def swap(value, axis, bit):
    return lax.ppermute(value, axis, [(i, i ^ bit) for i in range(lax.axis_size(axis))])


def to_plane(value, step):
    n = lax.axis_size("dp")
    return lax.ppermute(value, "dp", [(i, (i + 2 * step) % n) for i in range(n)])


def pick(value, index, axis=0):
    return lax.dynamic_index_in_dim(value, index, axis, keepdims=False)


def tuned():
    return (lax.axis_size("seq"), lax.axis_size("dp")) == (4, 8)


class Steps:
    def __init__(self):
        self.units = []

    def add(self, *units):
        self.units.extend([unit, None, None] for unit in units)
        return self.units[-len(units) :]

    def start(self, unit):
        (entry,) = self.add(unit)
        try:
            entry[1] = unit.send(None)
        except StopIteration as stop:
            entry[:] = [None, None, stop.value]
        return entry

    def tick(self, values=()):
        live = [u for u in self.units if u[0] is not None]
        waiting, values = lax.optimization_barrier(([u[1] for u in live], values))
        for unit, arrived in zip(live, waiting):
            try:
                unit[1] = unit[0].send(arrived)
            except StopIteration as stop:
                unit[:] = [None, None, stop.value]
        return values

    def drain(self):
        while any(u[0] is not None for u in self.units):
            self.tick()


def gather_unit(shard):
    d = lax.axis_index("dp")
    z, y = d // 2, d % 2
    arrived = yield [to_plane(shard, t) for t in (1, 2, 3)]
    column = jnp.stack([shard, *arrived])
    (other,) = yield [swap(column, "dp", 1)]
    both = jnp.concatenate([column, other], 0)
    chunks = [pick(both, ((k ^ y) * 4) + (z - j) % 4) for j in range(4) for k in (0, 1)]
    slab = jnp.concatenate(chunks, 0)
    near, across = yield [swap(slab, "seq", j) for j in (1, 2)]
    (far,) = yield [swap(across, "seq", 1)]
    return [slab, near, across, far]


def plain_gather(shard):
    return [lax.all_gather(shard, BOTH, axis=0, tiled=True)]
    yield


def gather(shard):
    return gather_unit(shard) if tuned() else plain_gather(shard)


def in_order(pieces):
    if not tuned():
        return pieces[0]
    s, every = lax.axis_index("seq"), jnp.stack(pieces)
    return jnp.concatenate([pick(every, s ^ j) for j in range(4)])


def scatter_unit(first, second, rows, waits):
    s, d = lax.axis_index("seq"), lax.axis_index("dp")
    high, low, y = d // 4, d // 2 % 2, d % 2
    wide, kind = rows * 8, BF

    def half(value, index):
        return pick(value.reshape(-1, 4, 2, rows, value.shape[-1]), index, 2).astype(F32)

    both = [f([s ^ 3, s ^ 1]) for f in (first, second)]
    ahead = [first([s ^ 2]), second([s ^ 2, s]), first([s])]
    if "join" in waits:
        both, *ahead = yield [swap(jnp.stack(both), "seq", 1), *ahead]
        one, two = both[0], both[1]
    else:
        one, two, *ahead = yield [*[swap(v, "seq", 1) for v in both], *ahead]
    for _ in range(waits.get("a", 0)):
        one, two, *ahead = yield [one, two, *ahead]
    across = (ahead[0].astype(F32) + one[:wide].astype(F32)).astype(kind)
    other = (half(ahead[1], 1 - y) + half(two, 1 - y)).astype(kind)
    sends = [swap(across, "seq", 2), swap(other, "dp", 1)]
    ahead = [
        (ahead[2].astype(F32) + one[wide:].astype(F32)).astype(kind),
        (half(ahead[1], y) + half(two, y)).astype(kind),
    ]
    across, beside, *ahead = yield [*sends, *ahead]
    for _ in range(waits.get("b", 0)):
        across, beside, *ahead = yield [across, beside, *ahead]
    other = (half(ahead[0], 1 - y) + half(across, 1 - y))[0].astype(kind)
    first_out = (ahead[1][0].astype(F32) + beside[0].astype(F32)).astype(kind)
    sends = [swap(other, "dp", 1), swap(first_out, "seq", 2)]
    ahead = [
        (half(ahead[0], y) + half(across, y))[0].astype(kind),
        (ahead[1][1].astype(F32) + beside[1].astype(F32)).astype(kind),
    ]
    *arrived, one, two = yield [*sends, *ahead]
    mine = [(a.astype(F32) + b.astype(F32)) for a, b in zip((one, two), arrived)]
    mine = [v.reshape(2, 2, *v.shape[1:]) for v in mine]
    other = jnp.stack([pick(v, 1 - low, 1) for v in mine], 1).astype(kind)
    own = jnp.stack([pick(v, low, 1) for v in mine], 1).astype(kind)
    far, own = yield [swap(other, "dp", 2), own]
    for _ in range(waits.get("high", 0)):
        far, own = yield [far, own]
    other = (pick(own, 1 - high).astype(F32) + pick(far, 1 - high).astype(F32)).astype(kind)
    own = pick(own, high).astype(F32) + pick(far, high).astype(F32)
    far, own = yield [swap(other, "dp", 4), own]
    total = own + far.astype(F32)
    return [total[0], total[1]]


def plain_scatter(*wholes):
    results = []
    for whole in wholes:
        part = lax.psum_scatter(whole, "seq", scatter_dimension=0, tiled=True)
        results.append(lax.psum_scatter(part, "dp", scatter_dimension=0, tiled=True))
    return results
    yield


def scatter(*pairs, waits={}):
    if not tuned():
        return plain_scatter(*[product_t(left, grad) for left, grad in pairs])

    def blocks(left, grad, start, width):
        def block(shards, *added):
            return slab_grad(left, grad, left.shape[1] // 4, start, width, shards, added)

        return block

    if len(pairs) == 1:
        left, grad = pairs[0]
        half = grad.shape[1] // 2
        pairs = ((left, grad, 0, half), (left, grad, half, half))
    else:
        pairs = [(left, grad, 0, grad.shape[1]) for left, grad in pairs]
    rows = pairs[0][0].shape[1] // 4 // lax.axis_size("dp")
    return scatter_unit(*[blocks(*pair) for pair in pairs], rows, waits)


def renew(weight, moment, average, grad, factor, tokens):
    rate = factor / math.sqrt(tokens)
    moment = 0.9 * moment + grad
    weight = weight - rate * (grad + 0.9 * moment)
    average = 0.8 * average + 0.2 * weight
    return (weight, moment, average)


def local(block_input, out_grad, lengths, *state):
    params, moments, averages = state[0::3], state[1::3], state[2::3]
    vectors, mix_weights, ffn_key, ffn_recept, ffn_value, maa_down, maa_up, decay_down, decay_up = params
    length, width = block_input.shape[1:]
    tokens = length * lax.axis_size("seq") * lax.axis_size("dp")
    rank = maa_up.shape[1]
    n_vec, n_down, n_decay = vectors.shape[0], maa_down.shape[1], decay_down.shape[1]
    start = lengths[0, 0] - lax.axis_index("seq") * length
    follows = (jnp.arange(length) != start) & (
        (jnp.arange(length) > 0) | (lax.axis_index("seq") > 0)
    )
    follows = follows.astype(F32)[:, None]
    keep = (jnp.arange(length // CHUNK) * CHUNK != start).astype(F32)

    small = jnp.concatenate(
        [vectors.T, maa_down, maa_up.reshape(5 * rank, -1).T, decay_down, decay_up.T], axis=1
    )
    ups = Steps()
    (small,) = ups.add(gather(small))
    square = jnp.concatenate([mix_weights, ffn_recept[None]]).astype(BF)
    square = lax.all_gather(square, BOTH, axis=1, tiled=True)
    fkey = lax.all_gather(ffn_key.astype(BF), BOTH, axis=0, tiled=True)
    fval = lax.all_gather(ffn_value.astype(BF), BOTH, axis=0, tiled=True)
    mix, wout, frec = square[:4], square[4], square[5]
    ups.drain()
    small = in_order(small[-1])
    cuts = np.cumsum([n_vec, n_down, 5 * rank, n_decay, n_decay])
    vecs, down, up, ddown, dup = jnp.split(small, cuts[:-1], axis=1)
    vecs, up, dup = vecs.T, up.T, dup.T

    hidden = block_input[0].astype(F32)
    normed, pull_norm_one = jax.vjp(norm_first, hidden, vecs)
    incoming = send_rows(normed)
    up = up.reshape(5, rank, width)
    prior = shifted(normed, incoming, follows)
    (xkey, xval, xrec, xgate), logdec, lora, tan = mix_inputs(
        normed, prior, vecs, down, up, ddown, dup
    )
    keys = product(xkey, mix[0])
    values = product(xval, mix[1])
    closing, carry = close(keep, keys, values, logdec)
    before = prefix(carry, closing, False)
    recept = product(xrec, mix[2])
    gate = product(xgate, mix[3])
    vec3 = vecs[9:12]
    raw, gated, score, states = forward(keep, recept, keys, values, logdec, gate, vec3, before)
    middle = hidden + product(gated, wout)

    second, pull_norm_two = jax.vjp(norm_second, middle, vecs)
    incoming_two = send_rows(second)
    (key_in, rec_in), pull_channel = jax.vjp(
        functools.partial(channel_inputs, follows=follows), second, incoming_two, vecs
    )
    key_in, rec_in = key_in.astype(BF), rec_in.astype(BF)
    positive = jnp.maximum(product(key_in, fkey), 0.0)
    squared = (positive * positive).astype(BF)
    sigma = jax.nn.sigmoid(product(rec_in, frec))
    squared, positive, sigma = lax.optimization_barrier((squared, positive, sigma))
    kvals = product(squared, fval)
    block_output = middle + sigma * kvals

    steps = Steps()
    upstream = out_grad[0].astype(F32)
    grad_kvals = (upstream * sigma).astype(BF)
    grad_rpre = (upstream * kvals * sigma * (1.0 - sigma)).astype(BF)
    (sum_fval,) = steps.add(scatter((squared, grad_kvals), waits={"b": 1, "high": 1}))
    grad_kvals = steps.tick(grad_kvals)
    grad_kpre = back_dot(grad_kvals, fval, positive=positive)
    grad_kpre = steps.tick(grad_kpre)
    grad_second, grad_inc_two, vec_one = pull_channel(
        (back_dot(grad_kpre, fkey), back_dot(grad_rpre, square, 5))
    )
    grad_second = back_rows(grad_inc_two, grad_second)
    grad_mid, vec_two = pull_norm_two(grad_second)
    grad_middle = upstream + grad_mid
    grad_attn = grad_middle.astype(BF)
    grad_attn, key_in, grad_kpre = lax.optimization_barrier((grad_attn, key_in, grad_kpre))
    (sum_fkey,) = steps.add(scatter((key_in, grad_kpre), waits={"a": 1}))
    grad_attn, rec_in, grad_rpre = steps.tick((grad_attn, rec_in, grad_rpre))
    sum_rec_out = steps.start(
        scatter((rec_in, grad_rpre), (gated, grad_attn), waits={"high": 2})
    )
    grad_gated = back_dot(grad_attn, square, 4)
    grad_raw, grad_gate, direct, vec_head = head_back(
        keep, recept, logdec, raw, gate, grad_gated, vec3
    )
    later = prefix(carry, direct, True)
    later, grad_gate = steps.tick((later, grad_gate))
    grad_rec, grad_key, grad_val, grad_dec, vec_bonus = backward(
        keep, recept, keys, values, logdec, grad_raw, score, states, later, vec3
    )
    grads = (grad_key, grad_val, grad_rec, grad_gate)
    grads, grad_dec = steps.tick((grads, grad_dec))
    grad_key, grad_val, grad_rec, grad_gate = grads
    mixed = mix_back(
        [back_dot(grad, square, i) for i, grad in enumerate(grads)],
        grad_dec, logdec, normed, prior, follows, vecs, lora, tan, down, up, ddown, dup,
    )
    mixed, grads = steps.tick((mixed, grads))
    grad_key, grad_val, grad_rec, grad_gate = grads
    sum_gate_rec = steps.start(
        scatter((xgate, grad_gate), (xrec, grad_rec), waits={"join": 1})
    )
    sum_key_val = steps.start(
        scatter((xkey, grad_key), (xval, grad_val), waits={"join": 1, "a": 1})
    )
    mixed = steps.tick(mixed)
    grad_normed, grad_inc, vec_mix, gdown, gup, gddown, gdup = mixed
    grad_normed = back_rows(grad_inc, grad_normed)
    grad_hidden, vec_three = pull_norm_one(grad_normed)
    input_grad = grad_middle + grad_hidden

    vec_all = vec_one + vec_two + vec_three
    vec_all = jnp.concatenate(
        [vec_all[:2], vec_mix[:7], vec_bonus, vec_head, vec_all[12:]], axis=0
    )
    total = jnp.concatenate(
        [vec_all.T, gdown, gup.reshape(5 * rank, width).T, gddown, gdup.T], axis=1
    )
    total, input_grad = steps.tick((total, input_grad))
    total = lax.psum_scatter(total, "seq", scatter_dimension=0, tiled=True)
    total = steps.tick(total)
    total = lax.psum_scatter(total, "dp", scatter_dimension=0, tiled=True)
    steps.drain()

    gvec, gdown, gup, gddown, gdup = jnp.split(total, cuts[:-1], axis=1)
    grad_frec, grad_out = sum_rec_out[-1]
    grads = (
        gvec.T,
        jnp.stack([*sum_key_val[-1], sum_gate_rec[-1][1], sum_gate_rec[-1][0], grad_out]),
        jnp.concatenate(sum_fkey[-1], 1),
        grad_frec,
        jnp.concatenate(sum_fval[-1], 1),
        gdown,
        gup.T.reshape(maa_up.shape),
        gddown,
        gdup.T,
    )
    results = [block_output[None], input_grad[None]]
    for param, moment, average, grad, factor in zip(params, moments, averages, grads, FACTORS):
        results.extend(renew(param, moment, average, grad, factor, tokens))
    return tuple(results)


def solution(mesh):
    vec, mix = P(None, BOTH), P(None, BOTH, None)
    rows, up = P(BOTH, None), P(None, None, BOTH)
    specs = [vec, mix, rows, rows, rows, rows, up, rows, vec]
    state = tuple(spec for spec in specs for _ in range(3))
    tokens = P("dp", "seq", None)
    return jax.shard_map(
        local,
        mesh=mesh,
        in_specs=(tokens, tokens, P("dp", None)) + state,
        out_specs=(tokens, tokens) + state,
        check_vma=False,
    )
```
